256 devices in a mesh: vocab: 64 (over y, z, core), hid: 4 (over x).
Axes of the slice: x: 4, y: 4, z: 8, core: 2. Of those that a mesh axis runs over, the one named last changes fastest.
Arguments:
- hidden: bfloat16 [768, 4096], P('vocab', 'hid'), may hold values from -40 to 40
- head_weight: bfloat16 [151936, 4096], P('vocab', 'hid'), may hold values from -1 to 1
- teacher_ids: int32 [768, 64], replicated, may hold values from 0 to 151935, as said below
- teacher_probs: float32 [768, 64], replicated, may hold values from 0.001 to 0.03
- token_weight: float32 [768], replicated, may hold values from 16 to 256
Outputs:
- grad_hidden: bfloat16 [768, 4096], P('vocab', 'hid')
- grad_weight: bfloat16 [151936, 4096], P('vocab', 'hid')
The draws below stay inside these ranges and needn't reach their ends.
Inputs may be any that keep to these rules, and one draw needn't show every extreme that they name: `teacher_ids`: the 64 ids of a token are distinct.
All inputs are finite; a program needn't handle non-finite values.
Results may differ from the reference program's by a relative error of at most 0.0049.
Values may be sent and summed in bfloat16 or wider, within the bound.
A program may use at most 128 MiB of HBM per device.

```python
import math
import jax
import jax.numpy as jnp

V = 151936
D = 4096
TOPK = 64
TOKENS = 768


def unit_rows(key, row_ids):
    base_key = jax.random.fold_in(key, 11)

    def one_row(row_id):
        return jax.random.normal(jax.random.fold_in(base_key, row_id), (D,), jnp.float32)
    return jax.vmap(one_row)(row_ids) / math.sqrt(D)


def draw_head_weight(key, part):
    return unit_rows(key, jnp.arange(V, dtype=jnp.int32)).astype(jnp.bfloat16)


def draw_hidden(key, part):
    key = jax.random.fold_in(key, 5)
    key_list = jax.random.split(key, 1)
    values = jax.random.normal(key_list[0], (TOKENS, D), jnp.float32) * 3.5
    return jnp.clip(values, -40.0, 40.0).astype(jnp.bfloat16)


def draw_teacher_ids(key, part):
    key = jax.random.fold_in(key, 7)
    raw_ids = jax.random.randint(key, (TOKENS, TOPK), 0, V - TOPK + 1)
    raw_ids = raw_ids.at[0, 0].set(0).at[0, 1].set(V - TOPK)
    return (jnp.sort(raw_ids, axis=1) + jnp.arange(TOPK, dtype=jnp.int32)[None, :]).astype(jnp.int32)


def setup_inputs(seed: int = 0) -> dict:
    keys = jax.random.split(jax.random.key(seed), 6)
    return {
        "hidden": draw_hidden(jax.random.fold_in(keys[5], 71), 0),
        "head_weight": draw_head_weight(jax.random.fold_in(keys[5], 71), 0),
        "teacher_ids": draw_teacher_ids(jax.random.fold_in(keys[5], 71), 0),
        "teacher_probs": jnp.clip(jnp.exp(jax.random.uniform(keys[3], (TOKENS, TOPK), jnp.float32, math.log(0.001), math.log(0.03))), 0.001, 0.03),
        "token_weight": jnp.clip(jnp.exp(jax.random.uniform(keys[4], (TOKENS,), jnp.float32, math.log(16.0), math.log(256.0))), 16.0, 256.0),
    }


def reference(hidden, head_weight, teacher_ids, teacher_probs, token_weight):
    logits = jnp.dot(hidden, head_weight.T, preferred_element_type=jnp.float32)
    row_top = jnp.max(logits, axis=1)
    shifted = jnp.exp(logits - row_top[:, None])
    row_sum = jnp.sum(shifted, axis=1)
    row_index = jnp.arange(TOKENS, dtype=jnp.int32)[:, None]
    target = jnp.zeros((TOKENS, V), jnp.float32).at[row_index, teacher_ids].add(teacher_probs)
    teacher_mass = jnp.sum(teacher_probs, axis=1)
    grad_logits = (token_weight[:, None] * (teacher_mass[:, None] * shifted / row_sum[:, None] - target)).astype(jnp.bfloat16)
    grad_hidden = jnp.dot(grad_logits, head_weight, preferred_element_type=jnp.float32).astype(jnp.bfloat16)
    grad_weight = jnp.dot(grad_logits.T, hidden, preferred_element_type=jnp.float32).astype(jnp.bfloat16)
    return grad_hidden, grad_weight
```

```python
import functools

import jax
import jax.numpy as jnp
from jax import lax
from jax.experimental import pallas as pl
from jax.experimental.pallas import tpu as pltpu
from jax.sharding import PartitionSpec as P

MESH = pl.DeviceIdType.MESH
F32, BF16 = jnp.float32, jnp.bfloat16
NX, NY, NZ, NC = 4, 4, 8, 2
TOK, TOPK = 768, 64
NG, GT = 3, 256
VL, QR, BR = 2374, 608, 304
VP = NX * QR
DW = 1024
HD = DW // 2


def remote(src, dst, sems, index, device):
    return pltpu.make_async_remote_copy(
        src_ref=src, dst_ref=dst, send_sem=sems.at[(0, *index)], recv_sem=sems.at[(1, *index)],
        device_id=device, device_id_type=MESH,
    )


def kernel(
    hid_ref, w_ref, tail_ref, ids_ref, probs_ref, tw_ref, gw_ref, gh_ref,
    wv, wq, hp, hc, ex, tgt, st, stt, gw, gp, cb, ysum, yb, zsum, zb, fin, finb, outf,
    sown, sx, scr, sz, sy, fac,
    wl_sem, hl_sem, go_sem, xs, ws, ays, azs, bzs, bys, acs, bcs, es, fs, sxs, scs, szs, sys_, r1s, r2s, r3s, r4s,
):
    v = lax.axis_index("vocab")
    x = lax.axis_index("hid")
    y, z, c = v // (NZ * NC), lax.rem(v // NC, NZ), lax.rem(v, NC)

    def to(dx=0, dy=0, dz=0, dc=0):
        nx, ny = lax.rem(x + dx + NX, NX), lax.rem(y + dy + NY, NY)
        nz, nc = lax.rem(z + dz + NZ, NZ), lax.rem(c + dc, NC)
        return ((ny * NZ + nz) * NC + nc, nx)

    def px(d):
        return lax.rem(x + d + NX, NX)

    def py(d):
        return lax.rem(y + d + NY, NY)

    def pz(d):
        return lax.rem(z + d + NZ, NZ)

    pending = []

    def go(copy):
        copy.start()
        pending.append(copy)

    loads = []
    for k in range(NX):
        rows = QR if k < NX - 1 else 2368 - 3 * QR
        copy = pltpu.make_async_copy(w_ref.at[pl.ds(k * QR, rows)], wv.at[pl.ds(k * QR, rows)], wl_sem.at[k])
        copy.start()
        loads.append(copy)
    copy = pltpu.make_async_copy(tail_ref, wv.at[pl.ds(2368, 64)], wl_sem.at[NX])
    copy.start()
    loads.append(copy)

    def place_a(cc, zz, yy):
        return ((cc * NZ + zz) * NY + yy) * 2

    def place_b(cc, yy, zz):
        return 128 + ((cc * NY + yy) * NZ + zz) * 2

    def place(q):
        return jnp.where(q < 2, place_a(c, z, y), place_b(c, y, z)) + lax.rem(q, 2)

    own = pltpu.make_async_copy(hid_ref, hp.at[place(x)], hl_sem.at[0])
    own.start()

    peers = [dict(dx=d) for d in (1, 2, 3)] + [dict(dy=d) for d in (1, 2, 3)]
    peers += [dict(dz=d) for d in range(1, NZ)] + [dict(dc=1)]
    barrier = pltpu.get_barrier_semaphore()
    for peer in peers:
        pl.semaphore_signal(barrier, inc=1, device_id=to(**peer), device_id_type=MESH)
    pl.semaphore_wait(barrier, len(peers))

    for d in (1, 2, 3):
        go(remote(hid_ref, hp.at[place(x)], xs, (d - 1,), to(dx=d)))
    for copy in loads:
        copy.wait()

    def w_copy(b, d):
        q = px(d)
        return remote(
            wv.at[pl.ds(pl.multiple_of(q * QR + b * BR, 16), BR)], wq.at[d - 1, pl.ds(b * BR, BR)],
            ws, (b, d - 1), to(dx=d),
        )

    for b in range(2):
        for d in (1, 3, 2):
            go(w_copy(b, d))

    anchor = v * VL
    tw = tw_ref[...]

    def target(lo, hi):
        @pl.loop(lo * 6, hi * 6)
        def _(i):
            rows = pl.ds(pl.multiple_of((i // 6) * 128, 128), 128)
            lanes = pl.ds(pl.multiple_of(lax.rem(i, 6) * 128, 128), 128)
            index = lax.broadcasted_iota(jnp.int32, (128, 128), 0) + (anchor + (i // 6) * 128)
            total = jnp.zeros((128, 128), F32)
            for k in range(TOPK):
                total = jnp.where(ids_ref[pl.ds(k, 1), lanes] == index, probs_ref[pl.ds(k, 1), lanes], total)
            tgt[rows, lanes] = total * tw_ref[pl.ds(0, 1), lanes]

    target(0, 2)

    own.wait()
    for d in (1, 2, 3):
        at = hp.at[place(px(-d))]
        remote(at, at, xs, (d - 1,), to(dx=d)).wait_recv()

    def block(start, size):
        return hp.at[pl.ds(start, size)]

    def ay(dd, d):
        at = block(place_a(c, z, py(dd)), 2)
        return remote(at, at, ays, (d - 1,), to(dy=d))

    def az(origin, way, s):
        at = block(place_a(c, pz(origin), 0), 8)
        return remote(at, at, azs, (way, s - 1), to(dz=1 if way == 0 else -1))

    def bz(origin, way, s):
        at = block(place_b(c, y, pz(origin)), 2)
        return remote(at, at, bzs, (way, s - 1), to(dz=1 if way == 0 else -1))

    def by(dd, d):
        at = block(place_b(c, py(dd), 0), 16)
        return remote(at, at, bys, (d - 1,), to(dy=d))

    def ac(k, cc):
        at = block(place_a(cc, pz(k), 0), 8)
        return remote(at, at, acs, (k,), to(dc=1))

    def bc(k, cc):
        at = block(place_b(cc, py(k), 0), 16)
        return remote(at, at, bcs, (k,), to(dc=1))

    for d in (1, 3, 2):
        go(ay(0, d))
    go(bz(0, 0, 1))
    go(bz(0, 1, 1))
    target(2, 4)
    for s in range(1, 5):
        for way, sign in ((0, -1), (1, 1)):
            if s <= (4, 3)[way]:
                bz(sign * s, way, s).wait_recv()
                if s < (4, 3)[way]:
                    go(bz(sign * s, way, s + 1))
        if s == 2:
            for d in (1, 2, 3):
                ay(-d, d).wait_recv()
            go(az(0, 0, 1))
            go(az(0, 1, 1))
            go(ac(0, c))
        if s < 4:
            target(3 + s, 4 + s)
    for d in (1, 3, 2):
        go(by(0, d))
    go(bc(0, c))
    target(7, 9)
    for s in range(1, 5):
        for way, sign in ((0, -1), (1, 1)):
            if s <= (4, 3)[way]:
                az(sign * s, way, s).wait_recv()
                if s < (4, 3)[way]:
                    go(az(sign * s, way, s + 1))
                go(ac((sign * s) % NZ, c))
        if s < 4:
            target(8 + 2 * s - 1, 8 + 2 * s + 1)
    for d in (1, 3, 2):
        by(-d, d).wait_recv()
        go(bc((-d) % NY, c))
    target(15, 19)
    for k in range(NZ):
        ac(k, 1 - c).wait_recv()
    for k in range(NY):
        bc(k, 1 - c).wait_recv()

    row = lax.broadcasted_iota(jnp.int32, (3 * 64, 256), 0)
    col = lax.broadcasted_iota(jnp.int32, (3 * 64, 256), 1)
    g_, i_ = row // 64, lax.rem(row, 64)
    pick = lax.rem(i_ // 4, 2) * 128 + (i_ // 8) * 16 + 4 * g_ + lax.rem(i_, 4)
    perm = jnp.where(col == pick, 1.0, 0.0).astype(BF16)

    @pl.loop(0, NX * NY)
    def _(i):
        q, yy = i // NY, lax.rem(i, NY)
        parts = []
        for cc in range(NC):
            for zz in range(NZ):
                at = jnp.where(q < 2, place_a(cc, zz, yy), place_b(cc, yy, zz)) + lax.rem(q, 2)
                parts.append(hp[at])
        rows = jnp.dot(perm, jnp.concatenate(parts, axis=0), preferred_element_type=F32).astype(BF16)
        for g in range(NG):
            hc[q, pl.ds(pl.multiple_of(g * GT + yy * 64, 16), 64), :] = rows[g * 64:(g + 1) * 64]

    def logits(b):
        for d in (1, 2, 3):
            w_copy_recv = remote(
                wq.at[d - 1, pl.ds(b * BR, BR)], wq.at[d - 1, pl.ds(b * BR, BR)], ws, (b, d - 1), to(dx=d)
            )
            w_copy_recv.wait_recv()
        first = x * QR + b * BR

        @pl.loop(0, NG)
        def _(g):
            toks = pl.ds(pl.multiple_of(g * GT, GT), GT)
            nt = (((1,), (1,)), ((), ()))
            total = lax.dot_general(
                wv[pl.ds(pl.multiple_of(first, 16), BR), :], hc[x, toks, :], nt, preferred_element_type=F32
            )
            for d in (1, 2, 3):
                total += lax.dot_general(
                    wq[d - 1, pl.ds(b * BR, BR), :], hc[px(-d), toks, :], nt, preferred_element_type=F32
                )
            real = lax.broadcasted_iota(jnp.int32, (BR, GT), 0) + first < VL
            total = jnp.where(real, total, -1e30)
            top = jnp.max(total, axis=0, keepdims=True)
            shifted = jnp.exp(total - top)
            sown[pl.ds(b, 1), toks] = top
            sown[pl.ds(2 + b, 1), toks] = jnp.sum(shifted, axis=0, keepdims=True)
            ex[x, b, g] = shifted.astype(BF16)

    def e_copy(q, b, g, way):
        at = ex.at[q, b, g]
        return remote(at, at, es, (way, b, g), to(dx=1 if way == 0 else -1))

    def f_copy(q, b, g):
        at = ex.at[q, b, g]
        return remote(at, at, fs, (b, g), to(dx=1 if b == 0 else -1))

    def e_send(b, g):
        go(e_copy(x, b, g, 0))
        go(e_copy(x, b, g, 1))

    def e_forward(g):
        for b in range(2):
            e_copy(px(-1), b, g, 0).wait_recv()
            if b == 0:
                go(f_copy(px(-1), 0, g))
        for b in (1, 0):
            e_copy(px(1), b, g, 1).wait_recv()
            if b == 1:
                go(f_copy(px(1), 1, g))

    sown[...] = jnp.zeros_like(sown)
    logits(0)
    e_send(0, 0)
    e_send(0, 1)
    logits(1)

    def sx_copy(q, d):
        return remote(sown, sx.at[q], sxs, (d - 1,), to(dx=d))

    for d in (1, 3, 2):
        go(sx_copy(x, d))
    e_send(1, 0)
    e_send(1, 1)
    sx[x] = sown[...]
    for d in (1, 3, 2):
        sx_copy(px(-d), d).wait_recv()
    tops = [sx[q, pl.ds(b, 1), :] for q in range(NX) for b in range(2)]
    sums = [sx[q, pl.ds(2 + b, 1), :] for q in range(NX) for b in range(2)]

    def merge(tops, sums):
        top = functools.reduce(jnp.maximum, tops)
        return top, functools.reduce(jnp.add, [s * jnp.exp(t - top) for s, t in zip(sums, tops)])

    def spread(buf, sems, me, top, total, moves, slot):
        buf[me] = jnp.zeros((8, TOK), F32)
        buf[me, pl.ds(0, 1), :] = top
        buf[me, pl.ds(1, 1), :] = total
        for i, move in enumerate(moves):
            go(remote(buf.at[me], buf.at[me], sems, (i,), to(**move)))
        for i, move in enumerate(moves):
            at = buf.at[slot(move)]
            remote(at, at, sems, (i,), to(**move)).wait_recv()
        n = len(moves) + 1
        return merge([buf[k, pl.ds(0, 1), :] for k in range(n)], [buf[k, pl.ds(1, 1), :] for k in range(n)])

    top, total = merge(tops, sums)
    top, total = spread(scr, scs, c, top, total, [dict(dc=1)], lambda m: 1 - c)
    top, total = spread(sz, szs, z, top, total, [dict(dz=d) for d in range(1, NZ)], lambda m: pz(-m["dz"]))
    e_forward(0)
    e_send(0, 2)
    e_send(1, 2)
    top, total = spread(sy, sys_, y, top, total, [dict(dy=d) for d in range(1, NY)], lambda m: py(-m["dy"]))
    scale = tw * jnp.sum(probs_ref[...], axis=0, keepdims=True) / total
    for i in range(2 * NX):
        fac[pl.ds(i, 1), :] = scale * jnp.exp(tops[i] - top)
    e_forward(1)

    def scores(g):
        f_copy(px(2), 0, g).wait_recv()
        f_copy(px(2), 1, g).wait_recv()
        toks = pl.ds(g * GT, GT)

        @pl.loop(0, 2 * NX)
        def _(i):
            rows = pl.ds(pl.multiple_of(i * BR, 16), BR)
            e = ex[i // 2, lax.rem(i, 2), g].astype(F32)
            st[rows, :] = (fac[pl.ds(i, 1), toks] * e - tgt[rows, toks]).astype(BF16)

        @pl.loop(0, VP // 128)
        def _(i):
            at = pl.ds(pl.multiple_of(i * 128, 128), 128)
            stt[:, at] = st[at, :].T

        @pl.loop(0, DW // 256)
        def _(i):
            at = pl.ds(pl.multiple_of(i * 256, 256), 256)
            gp[g, :, at] = jnp.dot(stt[...], wv[:, at], preferred_element_type=F32)

    def half(cc):
        return pl.ds(pl.multiple_of(cc * HD, HD), HD)

    def r1(g, cc):
        return remote(gp.at[g, :, half(cc)], cb.at[g], r1s, (g,), to(dc=1))

    def r2(g, d):
        return remote(ysum.at[g, pl.ds(pl.multiple_of(py(d) * 64, 64), 64)], yb.at[g, d - 1], r2s, (g, d - 1), to(dy=d))

    def r3(g, d):
        return remote(zsum.at[g, pl.ds(pl.multiple_of(pz(d) * 8, 8), 8)], zb.at[g, d - 1], r3s, (g, d - 1), to(dz=d))

    def r4(g):
        return remote(fin.at[g], finb.at[g], r4s, (g,), to(dc=1))

    def start1(g):
        go(r1(g, 1 - c))

    def start2(g):
        r1(g, 1 - c).wait_recv()
        ysum[g] = gp[g, :, half(c)] + cb[g]
        for d in (1, 3, 2):
            go(r2(g, d))

    def start3(g):
        for d in (1, 3, 2):
            r2(g, d).wait_recv()
        zsum[g] = ysum[g, pl.ds(pl.multiple_of(y * 64, 64), 64), :] + yb[g, 0] + yb[g, 1] + yb[g, 2]
        for d in (1, 7, 2, 6, 3, 5, 4):
            go(r3(g, d))

    def start4(g):
        for d in range(1, NZ):
            r3(g, d).wait_recv()
        part = zsum[g, pl.ds(pl.multiple_of(z * 8, 8), 8), :]
        for d in range(1, NZ):
            part += zb[g, d - 1]
        fin[g] = part
        go(r4(g))

    def finish(g):
        r4(g).wait_recv()
        mine, other = fin[g], finb[g]
        left, right = jnp.where(c == 0, mine, other), jnp.where(c == 0, other, mine)
        for h, part in enumerate((left, right)):
            outf[pl.ds(4 * g, 4), pl.ds(h * HD, HD)] = jnp.where(c == 0, part[0:4], part[4:8])

    def gw_part(g, m):
        rows = pl.ds(m * QR, QR)
        part = jnp.dot(st[rows, :], hc[x, pl.ds(g * GT, GT), :], preferred_element_type=F32)
        if g == 0:
            gw[rows, :] = part
        elif g == 1:
            gw[rows, :] += part
        else:
            tiles = pl.ds(m * (QR // 16), QR // 16)
            hp[tiles] = (gw[rows, :] + part).astype(BF16).reshape(QR // 16, 16, DW)
            copy = pltpu.make_async_copy(hp.at[tiles], gw_ref.at[tiles], go_sem.at[m])
            copy.start()
            return copy

    scores(0)
    start1(0)
    for m in range(NX):
        gw_part(0, m)
    start2(0)
    e_forward(2)
    scores(1)
    start1(1)
    start3(0)
    for m in range(NX):
        gw_part(1, m)
    start2(1)
    start4(0)
    scores(2)
    start1(2)
    start3(1)
    for copy in pending:
        copy.wait_send()
    done = len(pending)
    outs = [gw_part(2, 0)]
    start2(2)
    outs.append(gw_part(2, 1))
    start4(1)
    start3(2)
    outs.append(gw_part(2, 2))
    finish(0)
    finish(1)
    outs.append(gw_part(2, 3))
    start4(2)
    finish(2)
    gh_ref[...] = outf[0:12, :].astype(BF16)
    for copy in outs:
        copy.wait()
    for copy in pending[done:]:
        copy.wait_send()


def local(hidden, head_weight, teacher_ids, teacher_probs, token_weight):
    def order(a):
        k = a.shape[1]
        return a.reshape(NY * NZ * NC, NG, 4, k).transpose(3, 1, 0, 2).reshape(k, TOK)

    hid = jnp.pad(hidden, ((0, 4), (0, 0)))
    tail = jnp.pad(head_weight[2368:], ((0, 58), (0, 0)))
    vmem, hbm = pl.BlockSpec(memory_space=pltpu.VMEM), pl.BlockSpec(memory_space=pl.ANY)
    dma = pltpu.SemaphoreType.DMA
    gw, gh = pl.pallas_call(
        kernel,
        out_shape=(
            jax.ShapeDtypeStruct((VP // 16, 16, DW), BF16),
            jax.ShapeDtypeStruct((12, DW), BF16),
        ),
        in_specs=[vmem, hbm, vmem, vmem, vmem, vmem],
        out_specs=(hbm, vmem),
        scratch_shapes=[
            pltpu.VMEM((VP, DW), BF16),
            pltpu.VMEM((3, QR, DW), BF16),
            pltpu.VMEM((256, 16, DW), BF16),
            pltpu.VMEM((NX, TOK, DW), BF16),
            pltpu.VMEM((NX, 2, NG, BR, GT), BF16),
            pltpu.VMEM((VP, TOK), F32),
            pltpu.VMEM((VP, GT), BF16),
            pltpu.VMEM((GT, VP), BF16),
            pltpu.VMEM((VP, DW), F32),
            pltpu.VMEM((NG, GT, DW), F32),
            pltpu.VMEM((NG, GT, HD), F32),
            pltpu.VMEM((NG, GT, HD), F32),
            pltpu.VMEM((NG, 3, 64, HD), F32),
            pltpu.VMEM((NG, 64, HD), F32),
            pltpu.VMEM((NG, 7, 8, HD), F32),
            pltpu.VMEM((NG, 8, HD), F32),
            pltpu.VMEM((NG, 8, HD), F32),
            pltpu.VMEM((16, DW), F32),
            pltpu.VMEM((8, TOK), F32),
            pltpu.VMEM((NX, 8, TOK), F32),
            pltpu.VMEM((NC, 8, TOK), F32),
            pltpu.VMEM((NZ, 8, TOK), F32),
            pltpu.VMEM((NY, 8, TOK), F32),
            pltpu.VMEM((8, TOK), F32),
            dma((5,)), dma((1,)), dma((4,)),
            dma((2, 3)), dma((2, 2, 3)), dma((2, 3)), dma((2, 2, 4)), dma((2, 2, 4)), dma((2, 3)), dma((2, 8)),
            dma((2, 4)), dma((2, 2, 2, 3)), dma((2, 2, 3)), dma((2, 3)), dma((2, 1)), dma((2, 7)), dma((2, 3)),
            dma((2, 3)), dma((2, 3, 3)), dma((2, 3, 7)), dma((2, 3)),
        ],
        compiler_params=pltpu.CompilerParams(
            collective_id=0, has_side_effects=True, vmem_limit_bytes=63 * 2**20
        ),
        name="head_backward",
    )(hid, head_weight, tail, order(teacher_ids), order(teacher_probs), order(token_weight[:, None]))
    return gh, gw.reshape(VP, DW)[:VL]


def solution(mesh):
    return jax.shard_map(
        local,
        mesh=mesh,
        in_specs=(P("vocab", "hid"), P("vocab", "hid"), P(), P(), P()),
        out_specs=(P("vocab", "hid"), P("vocab", "hid")),
        check_vma=False,
    )
```

```python
import functools

import jax
import jax.numpy as jnp
from jax import lax
from jax.experimental import pallas as pl
from jax.experimental.pallas import tpu as pltpu
from jax.sharding import PartitionSpec as P

MESH = pl.DeviceIdType.MESH
F32, BF16 = jnp.float32, jnp.bfloat16
NX, NY, NZ, NC = 4, 4, 8, 2
TOK, TOPK, UT = 768, 64, 128
GROUPS = ((0, 2, 4, 0), (2, 2, 4, 4), (4, 1, 2, 8), (5, 1, 2, 10))
NG = len(GROUPS)
VL, QR, BR = 2374, 608, 304
VP = NX * QR
DW = 1024
HD = DW // 2
PW = 768
NU = TOK // UT
NN, NT = (((1,), (0,)), ((), ())), (((1,), (1,)), ((), ()))


def dot(a, b, dims=NN):
    return lax.dot_general(a, b, dims, preferred_element_type=F32)


def remote(src, dst, sems, index, device):
    return pltpu.make_async_remote_copy(
        src_ref=src, dst_ref=dst, send_sem=sems.at[(0, *index)], recv_sem=sems.at[(1, *index)],
        device_id=device, device_id_type=MESH,
    )


def fold(a):
    return jnp.concatenate([a[:, u * UT:(u + 1) * UT] for u in range(NU)], axis=0)


def pieces(a):
    first = a.astype(BF16)
    rest = a - first.astype(F32)
    second = rest.astype(BF16)
    return first, second, (rest - second.astype(F32)).astype(BF16)


def kernel(
    hid_ref, edge_ref, w_ref, ids_ref, probs_ref, tw_ref, gw_ref, gh_ref,
    wv, wq, wt, pack, hp, hc, ex, tgt, st, gw, gp, cb, ysum, yb, zsum, zb, fin, finb, outf, ghs,
    sraw, sown, sx, scr, sz, sy, fac, idr, prr, twr, idp, wpp, vec,
    wl_sem, hl_sem, go_sem, xs, ws, ays, azs, bzs, bys, acs, bcs, es, fs, sxs, scs, szs, sys_, r1s, r2s, r3s, r4s,
):
    v = lax.axis_index("vocab")
    x = lax.axis_index("hid")
    y, z, c = v // (NZ * NC), lax.rem(v // NC, NZ), lax.rem(v, NC)

    def px(d):
        return lax.rem(x + d + NX, NX)

    def py(d):
        return lax.rem(y + d + NY, NY)

    def pz(d):
        return lax.rem(z + d + NZ, NZ)

    def to(dx=0, dy=0, dz=0, dc=0):
        return ((py(dy) * NZ + pz(dz)) * NC + lax.rem(c + dc, NC), px(dx))

    pending = []

    def go(copy):
        copy.start()
        pending.append(copy)

    loads = []
    for k in range(NX):
        rows = QR if k < NX - 1 else 2368 - 3 * QR
        loads.append(pltpu.make_async_copy(w_ref.at[pl.ds(k * QR, rows)], wv.at[pl.ds(k * QR, rows)], wl_sem.at[k]))
    smalls = [
        pltpu.make_async_copy(src, dst, hl_sem.at[i])
        for i, (src, dst) in enumerate(((ids_ref, idr), (probs_ref, prr), (tw_ref, twr)))
    ]
    for copy in loads + smalls:
        copy.start()

    def place_a(cc, zz, yy):
        return ((cc * NZ + zz) * NY + yy) * 2

    def place_b(cc, yy, zz):
        return 128 + ((cc * NY + yy) * NZ + zz) * 2

    def place(q):
        return jnp.where(q < 2, place_a(c, z, y), place_b(c, y, z)) + lax.rem(q, 2)

    pack[0:12, :] = hid_ref[:, 0:PW]
    for h in range(3):
        pack[12:16, 256 * h:256 * h + 256] = hid_ref[4 * h:4 * h + 4, PW:DW]
    hp[place(x)] = pack[...]
    edge = lax.broadcasted_iota(jnp.int32, (16, DW), 0) < VL - 2368
    wv[pl.ds(2368, 16), :] = jnp.where(edge, edge_ref[...], jnp.zeros((16, DW), BF16))
    wv[pl.ds(2384, 48), :] = jnp.zeros((48, DW), BF16)

    peers = [dict(dx=d) for d in (1, 2, 3)] + [dict(dy=d) for d in (1, 2, 3)]
    peers += [dict(dz=d) for d in range(1, NZ)] + [dict(dc=1)]
    barrier = pltpu.get_barrier_semaphore()
    for peer in peers:
        pl.semaphore_signal(barrier, inc=1, device_id=to(**peer), device_id_type=MESH)
    pl.semaphore_wait(barrier, len(peers))

    for d in (1, 2, 3):
        go(remote(pack, hp.at[place(x)], xs, (d - 1,), to(dx=d)))
    for copy in loads:
        copy.wait()

    def w_copy(b, d):
        q = px(d)
        return remote(
            wv.at[pl.ds(pl.multiple_of(q * QR + b * BR, 16), BR)], wq.at[d - 1, pl.ds(b * BR, BR)],
            ws, (b, d - 1), to(dx=d),
        )

    for b in range(2):
        for d in (1, 3, 2):
            go(w_copy(b, d))
    loaded = [pending.pop() for _ in range(6)]

    for copy in smalls:
        copy.wait()
    row = lax.broadcasted_iota(jnp.int32, (TOK, TOK), 0)
    col = lax.broadcasted_iota(jnp.int32, (TOK, TOK), 1)
    source = jnp.zeros((TOK, TOK), jnp.int32)
    for unit, units, per, first in GROUPS:
        i = col - unit * UT
        here = (i >= 0) & (i < units * UT)
        source = jnp.where(here, (i // per) * 12 + first + lax.rem(i, per), source)
    perm = jnp.where(row == source, 1.0, 0.0).astype(BF16)
    near = idr[...] - v * VL
    near = jnp.where((near >= 0) & (near < VL), near, 4095)
    low, high = (near & 255).astype(F32).astype(BF16), (near >> 8).astype(F32).astype(BF16)
    idp[...] = (dot(high, perm) * 256.0 + dot(low, perm)).astype(jnp.int32)
    probs = functools.reduce(jnp.add, [dot(a, perm) for a in pieces(prr[...])])
    tw = functools.reduce(jnp.add, [dot(a, perm) for a in pieces(twr[...].reshape(1, TOK))])
    wpp[...] = probs * tw
    vec[0:NU, :] = fold(tw * jnp.sum(probs, axis=0, keepdims=True))

    def target(lo, hi):
        @pl.loop(lo, hi)
        def _(i):
            rows = pl.ds(pl.multiple_of((i // 6) * BR, 16), BR)
            lanes = pl.ds(pl.multiple_of(lax.rem(i, 6) * 128, 128), 128)
            index = lax.broadcasted_iota(jnp.int16, (BR, 128), 0)
            total = jnp.zeros((BR, 128), BF16)
            for k in range(TOPK):
                here = (idp[pl.ds(k, 1), lanes] - (i // 6) * BR).astype(jnp.int16)
                mass = wpp[pl.ds(k, 1), lanes].astype(BF16)
                total = jnp.where(
                    jnp.broadcast_to(here, (BR, 128)) == index, jnp.broadcast_to(mass, (BR, 128)), total
                )
            tgt[rows, lanes] = total

    for d in (1, 2, 3):
        at = hp.at[place(px(-d))]
        remote(at, at, xs, (d - 1,), to(dx=d)).wait_recv()

    def block(start, size):
        return hp.at[pl.ds(start, size)]

    def ay(dd, d):
        at = block(place_a(c, z, py(dd)), 2)
        return remote(at, at, ays, (d - 1,), to(dy=d))

    def az(origin, way, s):
        at = block(place_a(c, pz(origin), 0), 8)
        return remote(at, at, azs, (way, s - 1), to(dz=1 if way == 0 else -1))

    def bz(origin, way, s):
        at = block(place_b(c, y, pz(origin)), 2)
        return remote(at, at, bzs, (way, s - 1), to(dz=1 if way == 0 else -1))

    def by(dd, d):
        at = block(place_b(c, py(dd), 0), 16)
        return remote(at, at, bys, (d - 1,), to(dy=d))

    def ac(k, cc):
        at = block(place_a(cc, pz(k), 0), 8)
        return remote(at, at, acs, (k,), to(dc=1))

    def bc(k, cc):
        at = block(place_b(cc, py(k), 0), 16)
        return remote(at, at, bcs, (k,), to(dc=1))

    def ring(make, s, cross=None):
        for way, sign, steps in ((0, -1, 4), (1, 1, 3)):
            if s <= steps:
                make(sign * s, way, s).wait_recv()
                if s < steps:
                    go(make(sign * s, way, s + 1))
                if cross is not None:
                    go(cross((sign * s) % NZ, c))

    for d in (1, 3, 2):
        go(ay(0, d))
    go(bz(0, 0, 1))
    go(bz(0, 1, 1))
    target(0, 5)
    ring(bz, 1)
    for d in (1, 2, 3):
        ay(-d, d).wait_recv()
    go(az(0, 0, 1))
    go(az(0, 1, 1))
    go(ac(0, c))
    target(5, 10)
    ring(bz, 2)
    target(10, 15)
    ring(bz, 3)
    ring(az, 1, ac)
    target(15, 20)
    ring(bz, 4)
    for d in (1, 3, 2):
        go(by(0, d))
    go(bc(0, c))
    target(20, 27)
    ring(az, 2, ac)
    target(27, 37)
    ring(az, 3, ac)
    target(37, 48)
    ring(az, 4, ac)
    for d in (1, 3, 2):
        by(-d, d).wait_recv()
        go(bc((-d) % NY, c))
    for k in range(NZ):
        ac(k, 1 - c).wait_recv()
    for k in range(NY):
        bc(k, 1 - c).wait_recv()

    kinds = [(per, first) for _, _, per, first in GROUPS]
    kinds += [(per, 12 + first % 4) for _, _, per, first in GROUPS]
    height = sum(16 * per for per, _ in kinds)
    row = lax.broadcasted_iota(jnp.int32, (height, 256), 0)
    col = lax.broadcasted_iota(jnp.int32, (height, 256), 1)
    pick = jnp.zeros((height, 256), jnp.int32)
    begins, start = [], 0
    for per, first in kinds:
        i = row - start
        here = (i >= 0) & (i < 16 * per)
        zz, rest = i // (2 * per), lax.rem(i, 2 * per)
        pick = jnp.where(here, (rest // per) * 128 + zz * 16 + first + lax.rem(rest, per), pick)
        begins.append(start)
        start += 16 * per
    perm = jnp.where(col == pick, 1.0, 0.0).astype(BF16)

    @pl.loop(0, NX * NY)
    def _(i):
        q, yy = i // NY, lax.rem(i, NY)
        parts = []
        for cc in range(NC):
            for zz in range(NZ):
                at = jnp.where(q < 2, place_a(cc, zz, yy), place_b(cc, yy, zz)) + lax.rem(q, 2)
                parts.append(hp[at])
        rows = dot(perm, jnp.concatenate(parts, axis=0)).astype(BF16)
        for g, (unit, _, per, first) in enumerate(GROUPS):
            n, h = 16 * per, 256 * (first // 4)
            here = pl.ds(pl.multiple_of(unit * UT + yy * n, 16), n)
            hc[q, here, 0:PW] = rows[begins[g]:begins[g] + n]
            hc[q, here, PW:DW] = rows[begins[NG + g]:begins[NG + g] + n, h:h + 256]

    def w_wait(b):
        for d in (1, 2, 3):
            at = wq.at[d - 1, pl.ds(b * BR, BR)]
            remote(at, at, ws, (b, d - 1), to(dx=d)).wait_recv()

    def logits(b):
        first = x * QR + b * BR

        @pl.loop(0, TOK // 256)
        def _(i):
            toks = pl.ds(pl.multiple_of(i * 256, 256), 256)
            total = dot(wv[pl.ds(pl.multiple_of(first, 16), BR), :], hc[x, toks, :], NT)
            for d in (1, 2, 3):
                total += dot(wq[d - 1, pl.ds(b * BR, BR), :], hc[px(-d), toks, :], NT)
            real = lax.broadcasted_iota(jnp.int32, (BR, 256), 0) + first < VL
            total = jnp.where(real, total, -1e30)
            top = jnp.max(total, axis=0, keepdims=True)
            shifted = jnp.exp(total - top)
            sraw[pl.ds(b, 1), toks] = top
            sraw[pl.ds(2 + b, 1), toks] = jnp.sum(shifted, axis=0, keepdims=True)
            shifted = shifted.astype(BF16)
            ex[x, b, 2 * i] = shifted[:, 0:128]
            ex[x, b, 2 * i + 1] = shifted[:, 128:256]

    def e_at(q, b, g):
        return ex.at[q, b, pl.ds(GROUPS[g][0], GROUPS[g][1])]

    def e_copy(q, b, g, way):
        at = e_at(q, b, g)
        return remote(at, at, es, (way, b, g), to(dx=1 if way == 0 else -1))

    def f_copy(q, b, g):
        at = e_at(q, b, g)
        return remote(at, at, fs, (b, g), to(dx=1 if b == 0 else -1))

    def e_send(b, g):
        go(e_copy(x, b, g, 0))
        go(e_copy(x, b, g, 1))

    def e_wait(b, g, way):
        e_copy(px(-1 if way == 0 else 1), b, g, way).wait_recv()

    def e_forward(b, g):
        e_wait(b, g, b)
        go(f_copy(px(-1 if b == 0 else 1), b, g))

    w_wait(0)
    logits(0)
    e_send(0, 0)
    @pl.loop(0, NX)
    def _(q):
        for i in range(0, QR, 128):
            n = min(128, QR - i)
            wt[q, :, i:i + n] = wv[pl.ds(pl.multiple_of(q * QR + i, 16), n), :].T

    w_wait(1)
    e_send(0, 1)
    logits(1)

    def sx_copy(q, d):
        return remote(sown, sx.at[q], sxs, (d - 1,), to(dx=d))

    for j in range(4):
        sown[j * NU:(j + 1) * NU, :] = fold(sraw[pl.ds(j, 1), :])
    for d in (1, 3, 2):
        go(sx_copy(x, d))
    e_send(1, 0)
    sx[x] = sown[...]
    e_forward(0, 0)
    e_send(1, 1)
    for d in (1, 3, 2):
        sx_copy(px(-d), d).wait_recv()
    tops = [sx[q, b * NU:(b + 1) * NU, :] for q in range(NX) for b in range(2)]
    sums = [sx[q, (2 + b) * NU:(3 + b) * NU, :] for q in range(NX) for b in range(2)]

    def merge(tops, sums):
        top = functools.reduce(jnp.maximum, tops)
        return top, functools.reduce(jnp.add, [s * jnp.exp(t - top) for s, t in zip(sums, tops)])

    def spread(buf, sems, me, top, total, moves, slot):
        buf[me] = jnp.zeros((16, UT), F32)
        buf[me, 0:NU, :] = top
        buf[me, NU:2 * NU, :] = total
        for i, move in enumerate(moves):
            go(remote(buf.at[me], buf.at[me], sems, (i,), to(**move)))
        for i, move in enumerate(moves):
            at = buf.at[slot(move)]
            remote(at, at, sems, (i,), to(**move)).wait_recv()
        n = len(moves) + 1
        return merge([buf[k, 0:NU, :] for k in range(n)], [buf[k, NU:2 * NU, :] for k in range(n)])

    top, total = merge(tops, sums)
    top, total = spread(scr, scs, c, top, total, [dict(dc=1)], lambda m: 1 - c)
    e_forward(1, 0)
    top, total = spread(sz, szs, z, top, total, [dict(dz=d) for d in range(1, NZ)], lambda m: pz(-m["dz"]))
    e_forward(0, 1)
    e_send(0, 2)
    e_send(1, 2)
    top, total = spread(sy, sys_, y, top, total, [dict(dy=d) for d in range(1, NY)], lambda m: py(-m["dy"]))
    scale = vec[0:NU, :] / total
    for i in range(2 * NX):
        fac[i, 0:NU, :] = scale * jnp.exp(tops[i] - top)

    def part(g, d):
        unit, units, _, _ = GROUPS[g]
        size = units * UT
        q = px(d)
        if d == 2:
            f_copy(q, 0, g).wait_recv()
            f_copy(q, 1, g).wait_recv()
        elif d != 0:
            e_wait(1 if d == -1 else 0, g, 0 if d == -1 else 1)
        base = q * QR
        for b in range(2):
            rows = pl.ds(pl.multiple_of(base + b * BR, 16), BR)
            for u in range(units):
                toks = pl.ds((unit + u) * UT, UT)
                e = ex[q, b, unit + u].astype(F32)
                score = fac[2 * q + b, pl.ds(unit + u, 1), :] * e - tgt[rows, toks].astype(F32)
                st[rows, u * UT:(u + 1) * UT] = score.astype(BF16)

        @pl.loop(0, 2)
        def _(i):
            at = pl.ds(pl.multiple_of(i * HD, HD), HD)
            term = dot(wt[q, at, :], st[pl.ds(pl.multiple_of(base, 16), QR), 0:size])
            if d == 0:
                gp[g][at, :] = term
            else:
                gp[g][at, :] += term

    def gw_part(g, d):
        unit, units, _, _ = GROUPS[g]
        size = units * UT
        rows = pl.ds(pl.multiple_of(px(d) * QR, 16), QR)
        term = dot(st[rows, 0:size], hc[x, pl.ds(unit * UT, size), :])
        if g == 0:
            gw[rows, :] = term
        elif g < NG - 1:
            gw[rows, :] += term
        else:
            wv[rows, :] = (gw[rows, :] + term).astype(BF16)
            copy = pltpu.make_async_copy(wv.at[rows], gw_ref.at[rows], go_sem.at[d % NX])
            copy.start()
            return copy

    def half(cc):
        return pl.ds(pl.multiple_of(cc * HD, HD), HD)

    def tall(g):
        return GROUPS[g][2] * 16

    def deep(g, zz):
        return pl.ds(pl.multiple_of((zz * GROUPS[g][2] * 2 // 8) * 8, 8), 8)

    def r1(g, cc):
        return remote(gp[g].at[half(cc)], cb[g], r1s, (g,), to(dc=1))

    def r2(g, d):
        n = tall(g)
        src = ysum[g].at[pl.ds(pl.multiple_of(py(d) * n, 8), n)]
        return remote(src, yb.at[g, d - 1, pl.ds(0, n)], r2s, (g, d - 1), to(dy=d))

    def r3(g, d):
        return remote(zsum.at[g, deep(g, pz(d))], zb.at[g, d - 1], r3s, (g, d - 1), to(dz=d))

    def r4(g):
        return remote(fin.at[g], finb.at[g], r4s, (g,), to(dc=1))

    def start1(g):
        go(r1(g, 1 - c))

    def start2(g):
        r1(g, 1 - c).wait_recv()
        ysum[g][...] = (gp[g][half(c), :] + cb[g][...]).T
        for d in (1, 3, 2):
            go(r2(g, d))

    def start3(g):
        n = tall(g)
        for d in (1, 3, 2):
            r2(g, d).wait_recv()
        mine = ysum[g][pl.ds(pl.multiple_of(y * n, 8), n), :]
        zsum[g, 0:n] = mine + yb[g, 0, 0:n] + yb[g, 1, 0:n] + yb[g, 2, 0:n]
        for d in (1, 7, 2, 6, 3, 5, 4):
            go(r3(g, d))

    def start4(g):
        for d in range(1, NZ):
            r3(g, d).wait_recv()
        term = zsum[g, deep(g, z), :]
        for d in range(1, NZ):
            term += zb[g, d - 1]
        fin[g] = term
        go(r4(g))

    def finish(g):
        _, _, per, first = GROUPS[g]
        r4(g).wait_recv()
        mine, other = fin[g], finb[g]
        left, right = jnp.where(c == 0, mine, other), jnp.where(c == 0, other, mine)
        for h, a in enumerate((left, right)):
            a = jnp.where(c == 0, a, jnp.concatenate([a[per:], a[:per]], axis=0))
            if per == 2:
                a = jnp.where(lax.rem(z, 2) == 0, a, jnp.concatenate([a[4:], a[:4]], axis=0))
            outf[first:first + per, h * HD:(h + 1) * HD] = a[:per]

    part(0, 0)
    e_forward(1, 1)
    part(0, -1)
    part(0, 1)
    part(0, 2)
    start1(0)
    e_send(0, 3)
    e_send(1, 3)
    for d in (0, -1, 1, 2):
        gw_part(0, d)
    part(1, 0)
    e_forward(0, 2)
    part(1, -1)
    part(1, 1)
    start2(0)
    e_forward(1, 2)
    part(1, 2)
    start1(1)
    for d in (0, -1, 1, 2):
        gw_part(1, d)
    e_forward(0, 3)
    e_forward(1, 3)
    part(2, 0)
    part(2, -1)
    part(2, 1)
    part(2, 2)
    start1(2)
    start2(1)
    for d in (0, -1, 1, 2):
        gw_part(2, d)
    part(3, 0)
    part(3, -1)
    part(3, 1)
    start3(0)
    start2(2)
    part(3, 2)
    start1(3)
    for copy in loaded:
        copy.wait_send()
    outs = [gw_part(3, 0)]
    start3(1)
    outs.append(gw_part(3, -1))
    start2(3)
    start4(0)
    outs.append(gw_part(3, 1))
    start3(2)
    start4(1)
    outs.append(gw_part(3, 2))
    finish(0)
    start3(3)
    start4(2)
    finish(1)
    start4(3)
    finish(2)
    finish(3)
    ghs[...] = outf[0:12, :].astype(BF16)
    outs.append(pltpu.make_async_copy(ghs, gh_ref, go_sem.at[NX]))
    outs[-1].start()
    for copy in outs:
        copy.wait()
    for copy in pending:
        copy.wait_send()


def results(gw_ref, gh_ref, gw_out, gh_out, sems):
    copies = [pltpu.make_async_copy(gh_ref, gh_out, sems.at[5])]
    for i, (start, rows) in enumerate(((0, QR), (QR, QR), (2 * QR, QR), (3 * QR, 2368 - 3 * QR), (2368, VL - 2368))):
        here = pl.ds(start, rows)
        copies.append(pltpu.make_async_copy(gw_ref.at[here], gw_out.at[here], sems.at[i]))
    for copy in copies:
        copy.start()
    for copy in copies:
        copy.wait()


def local(hidden, head_weight, teacher_ids, teacher_probs, token_weight):
    hbm = pl.BlockSpec(memory_space=pl.ANY)
    dma = pltpu.SemaphoreType.DMA
    gw, gh = pl.pallas_call(
        kernel,
        grid=(1,),
        out_shape=(pltpu.VMEM((VP, DW), BF16), pltpu.VMEM((12, DW), BF16)),
        in_specs=[
            pl.BlockSpec((12, DW), lambda i: (0, 0)),
            pl.BlockSpec((16, DW), lambda i: (2368 // 16, 0)),
            hbm, hbm, hbm, hbm,
        ],
        out_specs=(hbm, hbm),
        scratch_shapes=[
            pltpu.VMEM((VP, DW), BF16),
            pltpu.VMEM((3, QR, DW), BF16),
            pltpu.VMEM((NX, DW, QR), BF16),
            pltpu.VMEM((16, PW), BF16),
            pltpu.VMEM((256, 16, PW), BF16),
            pltpu.VMEM((NX, TOK, DW), BF16),
            pltpu.VMEM((NX, 2, TOK // UT, BR, UT), BF16),
            pltpu.VMEM((VP, TOK), BF16),
            pltpu.VMEM((VP, 256), BF16),
            pltpu.VMEM((VP, DW), F32),
            [pltpu.VMEM((DW, n * UT), F32) for _, n, _, _ in GROUPS],
            [pltpu.VMEM((HD, n * UT), F32) for _, n, _, _ in GROUPS],
            [pltpu.VMEM((n * UT, HD), F32) for _, n, _, _ in GROUPS],
            pltpu.VMEM((NG, 3, 64, HD), F32),
            pltpu.VMEM((NG, 64, HD), F32),
            pltpu.VMEM((NG, 7, 8, HD), F32),
            pltpu.VMEM((NG, 8, HD), F32),
            pltpu.VMEM((NG, 8, HD), F32),
            pltpu.VMEM((16, DW), F32),
            pltpu.VMEM((12, DW), BF16),
            pltpu.VMEM((8, TOK), F32),
            pltpu.VMEM((4 * NU, UT), F32),
            pltpu.VMEM((NX, 4 * NU, UT), F32),
            pltpu.VMEM((NC, 16, UT), F32),
            pltpu.VMEM((NZ, 16, UT), F32),
            pltpu.VMEM((NY, 16, UT), F32),
            pltpu.VMEM((2 * NX, 8, UT), F32),
            pltpu.VMEM((TOPK, TOK), jnp.int32),
            pltpu.VMEM((TOPK, TOK), F32),
            pltpu.VMEM((TOK,), F32),
            pltpu.VMEM((TOPK, TOK), jnp.int32),
            pltpu.VMEM((TOPK, TOK), F32),
            pltpu.VMEM((8, UT), F32),
            dma((4,)), dma((3,)), dma((5,)),
            dma((2, 3)), dma((2, 2, 3)), dma((2, 3)), dma((2, 2, 4)), dma((2, 2, 4)), dma((2, 3)), dma((2, 8)),
            dma((2, 4)), dma((2, 2, 2, NG)), dma((2, 2, NG)), dma((2, 3)), dma((2, 1)), dma((2, 7)), dma((2, 3)),
            dma((2, NG)), dma((2, NG, 3)), dma((2, NG, 7)), dma((2, NG)),
        ],
        compiler_params=pltpu.CompilerParams(
            collective_id=0, has_side_effects=True, vmem_limit_bytes=58 * 2**20
        ),
        name="head_backward",
    )(hidden, head_weight, head_weight, teacher_ids.T, teacher_probs.T, token_weight)
    gw, gh = pl.pallas_call(
        results,
        out_shape=(jax.ShapeDtypeStruct((VL, DW), BF16), jax.ShapeDtypeStruct((12, DW), BF16)),
        in_specs=[hbm, hbm],
        out_specs=(hbm, hbm),
        scratch_shapes=[dma((6,))],
        compiler_params=pltpu.CompilerParams(vmem_limit_bytes=2**20),
        name="results",
    )(gw, gh)
    return gh, gw


def solution(mesh):
    return jax.shard_map(
        local,
        mesh=mesh,
        in_specs=(P("vocab", "hid"), P("vocab", "hid"), P(), P(), P()),
        out_specs=(P("vocab", "hid"), P("vocab", "hid")),
        check_vma=False,
    )
```

```python
import functools

import jax
import jax.numpy as jnp
from jax import lax
from jax.experimental import pallas as pl
from jax.experimental.pallas import tpu as pltpu
from jax.sharding import PartitionSpec as P

MESH = pl.DeviceIdType.MESH
F32, BF16 = jnp.float32, jnp.bfloat16
NX, NY, NZ, NC = 4, 4, 8, 2
TOK, TOPK, UT = 768, 64, 128
GROUPS = ((0, 2, 4, 0), (2, 2, 4, 4), (4, 1, 2, 8), (5, 1, 2, 10))
NG = len(GROUPS)
VL, QR, BR = 2374, 608, 304
VP = NX * QR
DW = 1024
HD = DW // 2
PW = 768
NU = TOK // UT
NN, NT = (((1,), (0,)), ((), ())), (((1,), (1,)), ((), ()))


def dot(a, b, dims=NN):
    return lax.dot_general(a, b, dims, preferred_element_type=F32)


def remote(src, dst, sems, index, device):
    return pltpu.make_async_remote_copy(
        src_ref=src, dst_ref=dst, send_sem=sems.at[(0, *index)], recv_sem=sems.at[(1, *index)],
        device_id=device, device_id_type=MESH,
    )


def fold(a):
    return jnp.concatenate([a[:, u * UT:(u + 1) * UT] for u in range(NU)], axis=0)


def pieces(a):
    first = a.astype(BF16)
    rest = a - first.astype(F32)
    second = rest.astype(BF16)
    return first, second, (rest - second.astype(F32)).astype(BF16)


def kernel(
    hid_ref, edge_ref, w_ref, ids_ref, probs_ref, tw_ref, gw_ref, gh_ref,
    wv, wq, wta, wtb, pack, hp, hc, ex, tgt, st, gw, gp, cb, ysum, ysb, yb, zsum, zb, fin, finb, outf, ghs,
    sraw, sown, sx, scr, sz, sy, fac, idr, prr, twr, idp, wpp, vec,
    wl_sem, hl_sem, go_sem, xs, ws, ays, azs, bzs, bys, acs, bcs, es, fs, sxs, scs, szs, sys_, r1s, r2s, r3s, r4s,
):
    v = lax.axis_index("vocab")
    x = lax.axis_index("hid")
    y, z, c = v // (NZ * NC), lax.rem(v // NC, NZ), lax.rem(v, NC)

    def px(d):
        return lax.rem(x + d + NX, NX)

    slots = (0, -1, 1, 2)

    def py(d):
        return lax.rem(y + d + NY, NY)

    def pz(d):
        return lax.rem(z + d + NZ, NZ)

    def to(dx=0, dy=0, dz=0, dc=0):
        return ((py(dy) * NZ + pz(dz)) * NC + lax.rem(c + dc, NC), px(dx))

    pending = []

    def go(copy):
        copy.start()
        pending.append(copy)

    loads = []
    for k in range(NX):
        rows = QR if k < NX - 1 else 2368 - 3 * QR
        loads.append(pltpu.make_async_copy(w_ref.at[pl.ds(k * QR, rows)], wv.at[pl.ds(k * QR, rows)], wl_sem.at[k]))
    smalls = [
        pltpu.make_async_copy(src, dst, hl_sem.at[i])
        for i, (src, dst) in enumerate(((ids_ref, idr), (probs_ref, prr), (tw_ref, twr)))
    ]
    for copy in loads + smalls:
        copy.start()

    def place_a(cc, zz, yy):
        return ((cc * NZ + zz) * NY + yy) * 2

    def place_b(cc, yy, zz):
        return 128 + ((cc * NY + yy) * NZ + zz) * 2

    def place(q):
        return jnp.where(q < 2, place_a(c, z, y), place_b(c, y, z)) + lax.rem(q, 2)

    pack[0:12, :] = hid_ref[:, 0:PW]
    for h in range(3):
        pack[12:16, 256 * h:256 * h + 256] = hid_ref[4 * h:4 * h + 4, PW:DW]
    hp[place(x)] = pack[...]
    edge = lax.broadcasted_iota(jnp.int32, (16, DW), 0) < VL - 2368
    wv[pl.ds(2368, 16), :] = jnp.where(edge, edge_ref[...], jnp.zeros((16, DW), BF16))
    wv[pl.ds(2384, 48), :] = jnp.zeros((48, DW), BF16)

    peers = [dict(dx=d) for d in (1, 2, 3)] + [dict(dy=d) for d in (1, 2, 3)]
    peers += [dict(dz=d) for d in range(1, NZ)] + [dict(dc=1)]
    barrier = pltpu.get_barrier_semaphore()
    for peer in peers:
        pl.semaphore_signal(barrier, inc=1, device_id=to(**peer), device_id_type=MESH)
    pl.semaphore_wait(barrier, len(peers))

    for d in (1, 2, 3):
        go(remote(pack, hp.at[place(x)], xs, (d - 1,), to(dx=d)))
    for copy in loads:
        copy.wait()

    def w_copy(b, d):
        q = px(d)
        return remote(
            wv.at[pl.ds(pl.multiple_of(q * QR + b * BR, 16), BR)], wq.at[d - 1, pl.ds(b * BR, BR)],
            ws, (b, d - 1), to(dx=d),
        )

    for b in range(2):
        for d in (1, 3, 2):
            go(w_copy(b, d))
    loaded = [pending.pop() for _ in range(6)]

    for copy in smalls:
        copy.wait()
    row = lax.broadcasted_iota(jnp.int32, (TOK, TOK), 0)
    col = lax.broadcasted_iota(jnp.int32, (TOK, TOK), 1)
    source = jnp.zeros((TOK, TOK), jnp.int32)
    for unit, units, per, first in GROUPS:
        i = col - unit * UT
        here = (i >= 0) & (i < units * UT)
        source = jnp.where(here, (i // per) * 12 + first + lax.rem(i, per), source)
    perm = jnp.where(row == source, 1.0, 0.0).astype(BF16)
    near = idr[...] - v * VL
    near = jnp.where((near >= 0) & (near < VL), near, 4095)
    low, high = (near & 255).astype(F32).astype(BF16), (near >> 8).astype(F32).astype(BF16)
    idp[...] = (dot(high, perm) * 256.0 + dot(low, perm)).astype(jnp.int32)
    probs = functools.reduce(jnp.add, [dot(a, perm) for a in pieces(prr[...])])
    tw = functools.reduce(jnp.add, [dot(a, perm) for a in pieces(twr[...].reshape(1, TOK))])
    wpp[...] = probs * tw
    vec[0:NU, :] = fold(tw * jnp.sum(probs, axis=0, keepdims=True))

    def target(lo, hi):
        @pl.loop(lo, hi)
        def _(i):
            rows = pl.ds(pl.multiple_of((i // 6) * BR, 16), BR)
            lanes = pl.ds(pl.multiple_of(lax.rem(i, 6) * 128, 128), 128)
            index = lax.broadcasted_iota(jnp.int16, (BR, 128), 0)
            total = jnp.zeros((BR, 128), BF16)
            for k in range(TOPK):
                here = (idp[pl.ds(k, 1), lanes] - (i // 6) * BR).astype(jnp.int16)
                mass = wpp[pl.ds(k, 1), lanes].astype(BF16)
                total = jnp.where(
                    jnp.broadcast_to(here, (BR, 128)) == index, jnp.broadcast_to(mass, (BR, 128)), total
                )
            tgt[rows, lanes] = total

    for d in (1, 2, 3):
        at = hp.at[place(px(-d))]
        remote(at, at, xs, (d - 1,), to(dx=d)).wait_recv()

    def block(start, size):
        return hp.at[pl.ds(start, size)]

    def ay(dd, d):
        at = block(place_a(c, z, py(dd)), 2)
        return remote(at, at, ays, (d - 1,), to(dy=d))

    def az(origin, way, s):
        at = block(place_a(c, pz(origin), 0), 8)
        return remote(at, at, azs, (way, s - 1), to(dz=1 if way == 0 else -1))

    def bz(origin, way, s):
        at = block(place_b(c, y, pz(origin)), 2)
        return remote(at, at, bzs, (way, s - 1), to(dz=1 if way == 0 else -1))

    def by(dd, d):
        at = block(place_b(c, py(dd), 0), 16)
        return remote(at, at, bys, (d - 1,), to(dy=d))

    def ac(k, cc):
        at = block(place_a(cc, pz(k), 0), 8)
        return remote(at, at, acs, (k,), to(dc=1))

    def bc(k, cc):
        at = block(place_b(cc, py(k), 0), 16)
        return remote(at, at, bcs, (k,), to(dc=1))

    def ring(make, s, cross=None):
        for way, sign, steps in ((0, -1, 4), (1, 1, 3)):
            if s <= steps:
                make(sign * s, way, s).wait_recv()
                if s < steps:
                    go(make(sign * s, way, s + 1))
                if cross is not None:
                    go(cross((sign * s) % NZ, c))

    for d in (1, 3, 2):
        go(ay(0, d))
    go(bz(0, 0, 1))
    go(bz(0, 1, 1))
    target(0, 5)
    ring(bz, 1)
    for d in (1, 2, 3):
        ay(-d, d).wait_recv()
    go(az(0, 0, 1))
    go(az(0, 1, 1))
    go(ac(0, c))
    target(5, 10)
    ring(bz, 2)
    target(10, 15)
    ring(bz, 3)
    ring(az, 1, ac)
    target(15, 20)
    ring(bz, 4)
    for d in (1, 3, 2):
        go(by(0, d))
    go(bc(0, c))
    target(20, 27)
    ring(az, 2, ac)
    target(27, 37)
    ring(az, 3, ac)
    target(37, 48)
    ring(az, 4, ac)
    for d in (1, 3, 2):
        by(-d, d).wait_recv()
        go(bc((-d) % NY, c))
    for k in range(NZ):
        ac(k, 1 - c).wait_recv()
    for k in range(NY):
        bc(k, 1 - c).wait_recv()

    kinds = [(per, first) for _, _, per, first in GROUPS]
    kinds += [(per, 12 + first % 4) for _, _, per, first in GROUPS]
    height = sum(16 * per for per, _ in kinds)
    row = lax.broadcasted_iota(jnp.int32, (height, 256), 0)
    col = lax.broadcasted_iota(jnp.int32, (height, 256), 1)
    pick = jnp.zeros((height, 256), jnp.int32)
    begins, start = [], 0
    for per, first in kinds:
        i = row - start
        here = (i >= 0) & (i < 16 * per)
        zz, rest = i // (2 * per), lax.rem(i, 2 * per)
        pick = jnp.where(here, (rest // per) * 128 + zz * 16 + first + lax.rem(rest, per), pick)
        begins.append(start)
        start += 16 * per
    perm = jnp.where(col == pick, 1.0, 0.0).astype(BF16)

    @pl.loop(0, NX * NY)
    def _(i):
        q, yy = i // NY, lax.rem(i, NY)
        parts = []
        for cc in range(NC):
            for zz in range(NZ):
                at = jnp.where(q < 2, place_a(cc, zz, yy), place_b(cc, yy, zz)) + lax.rem(q, 2)
                parts.append(hp[at])
        rows = dot(perm, jnp.concatenate(parts, axis=0)).astype(BF16)
        for g, (unit, _, per, first) in enumerate(GROUPS):
            n, h = 16 * per, 256 * (first // 4)
            here = pl.ds(pl.multiple_of(unit * UT + yy * n, 16), n)
            hc[q, here, 0:PW] = rows[begins[g]:begins[g] + n]
            hc[q, here, PW:DW] = rows[begins[NG + g]:begins[NG + g] + n, h:h + 256]

    def w_wait(b):
        for d in (1, 2, 3):
            at = wq.at[d - 1, pl.ds(b * BR, BR)]
            remote(at, at, ws, (b, d - 1), to(dx=d)).wait_recv()

    def logits(b):
        first = x * QR + b * BR

        @pl.loop(0, TOK // 256)
        def _(i):
            toks = pl.ds(pl.multiple_of(i * 256, 256), 256)
            total = dot(wv[pl.ds(pl.multiple_of(first, 16), BR), :], hc[x, toks, :], NT)
            for d in (1, 2, 3):
                total += dot(wq[d - 1, pl.ds(b * BR, BR), :], hc[px(-d), toks, :], NT)
            real = lax.broadcasted_iota(jnp.int32, (BR, 256), 0) + first < VL
            total = jnp.where(real, total, -1e30)
            top = jnp.max(total, axis=0, keepdims=True)
            shifted = jnp.exp(total - top)
            sraw[pl.ds(b, 1), toks] = top
            sraw[pl.ds(2 + b, 1), toks] = jnp.sum(shifted, axis=0, keepdims=True)
            shifted = shifted.astype(BF16)
            ex[x, b, 2 * i] = shifted[:, 0:128]
            ex[x, b, 2 * i + 1] = shifted[:, 128:256]

    def e_at(q, b, g):
        return ex.at[q, b, pl.ds(GROUPS[g][0], GROUPS[g][1])]

    def e_copy(q, b, g, way):
        at = e_at(q, b, g)
        return remote(at, at, es, (way, b, g), to(dx=1 if way == 0 else -1))

    def f_copy(q, b, g):
        at = e_at(q, b, g)
        return remote(at, at, fs, (b, g), to(dx=1 if b == 0 else -1))

    def e_send(b, g):
        go(e_copy(x, b, g, 0))
        go(e_copy(x, b, g, 1))

    def e_wait(b, g, way):
        e_copy(px(-1 if way == 0 else 1), b, g, way).wait_recv()

    def e_forward(b, g):
        e_wait(b, g, b)
        go(f_copy(px(-1 if b == 0 else 1), b, g))

    w_wait(0)
    logits(0)
    for i in range(0, 3 * QR, 128):
        pieces_, j = [], i
        while j < min(i + 128, 3 * QR):
            k = j // QR
            n = min(i + 128, 3 * QR, (k + 1) * QR) - j
            pieces_.append(wv[pl.ds(pl.multiple_of(px(slots[k]) * QR + j - k * QR, 16), n), :])
            j += n
        wta[:, i:j] = jnp.concatenate(pieces_, axis=0).T
    for i in range(0, QR, 128):
        n = min(128, QR - i)
        wtb[:, i:i + n] = wv[pl.ds(pl.multiple_of(px(2) * QR + i, 16), n), :].T

    w_wait(1)
    e_send(0, 0)
    logits(1)

    def sx_copy(q, d):
        return remote(sown, sx.at[q], sxs, (d - 1,), to(dx=d))

    for j in range(4):
        sown[j * NU:(j + 1) * NU, :] = fold(sraw[pl.ds(j, 1), :])
    for d in (1, 3, 2):
        go(sx_copy(x, d))
    e_send(1, 0)
    sx[x] = sown[...]
    for d in (1, 3, 2):
        sx_copy(px(-d), d).wait_recv()
    tops = [sx[q, b * NU:(b + 1) * NU, :] for q in range(NX) for b in range(2)]
    sums = [sx[q, (2 + b) * NU:(3 + b) * NU, :] for q in range(NX) for b in range(2)]

    def merge(tops, sums):
        top = functools.reduce(jnp.maximum, tops)
        return top, functools.reduce(jnp.add, [s * jnp.exp(t - top) for s, t in zip(sums, tops)])

    def spread(buf, sems, me, top, total, moves, slot, between):
        buf[me] = jnp.zeros((16, UT), F32)
        buf[me, 0:NU, :] = top
        buf[me, NU:2 * NU, :] = total
        for i, move in enumerate(moves):
            go(remote(buf.at[me], buf.at[me], sems, (i,), to(**move)))
        between()
        for i, move in enumerate(moves):
            at = buf.at[slot(move)]
            remote(at, at, sems, (i,), to(**move)).wait_recv()
        n = len(moves) + 1
        return merge([buf[k, 0:NU, :] for k in range(n)], [buf[k, NU:2 * NU, :] for k in range(n)])

    e_forward(0, 0)
    top, total = merge(tops, sums)
    top, total = spread(scr, scs, c, top, total, [dict(dc=1)], lambda m: 1 - c, lambda: None)

    def between_z():
        e_forward(1, 0)
        e_send(0, 1)

    def between_y():
        e_send(1, 1)

    moves = [dict(dz=d) for d in (4, 3, 5, 2, 6, 1, 7)]
    top, total = spread(sz, szs, z, top, total, moves, lambda m: pz(-m["dz"]), between_z)
    moves = [dict(dy=d) for d in (2, 1, 3)]
    top, total = spread(sy, sys_, y, top, total, moves, lambda m: py(-m["dy"]), between_y)
    scale = vec[0:NU, :] / total
    for i in range(2 * NX):
        fac[i, 0:NU, :] = scale * jnp.exp(tops[i] - top)

    def part(g, far):
        unit, units, _, _ = GROUPS[g]
        size, lane = units * UT, (256, 0, 256, 384)[g]
        for k in (3,) if far else (0, 1, 2):
            q = px(slots[k])
            if k == 3:
                f_copy(q, 0, g).wait_recv()
                f_copy(q, 1, g).wait_recv()
            elif k != 0:
                e_wait(2 - k, g, k - 1)
            for b in range(2):
                rows = pl.ds(pl.multiple_of(q * QR + b * BR, 16), BR)
                for u in range(units):
                    toks = pl.ds((unit + u) * UT, UT)
                    e = ex[q, b, unit + u].astype(F32)
                    score = fac[2 * q + b, pl.ds(unit + u, 1), :] * e - tgt[rows, toks].astype(F32)
                    here = k * QR + b * BR
                    st[here:here + BR, lane + u * UT:lane + (u + 1) * UT] = score.astype(BF16)

        @pl.loop(0, 2)
        def _(i):
            at = pl.ds(pl.multiple_of(i * HD, HD), HD)
            if far:
                gp[g][at, :] += dot(wtb[at, :], st[3 * QR:VP, lane:lane + size])
            else:
                gp[g][at, :] = dot(wta[at, :], st[0:3 * QR, lane:lane + size])

    def gw_part(g, k):
        rows = slice(k * QR, (k + 1) * QR)
        if g == 0:
            gw[rows, :] = dot(st[rows, 256:512], hc[x, 0:256, :])
        else:
            term = dot(st[rows, :], hc[x, 256:TOK, :])
            wv[rows, :] = (gw[rows, :] + term).astype(BF16)
            there = pl.ds(pl.multiple_of(px(slots[k]) * QR, 16), QR)
            copy = pltpu.make_async_copy(wv.at[pl.ds(k * QR, QR)], gw_ref.at[there], go_sem.at[k])
            copy.start()
            return copy

    def half(cc):
        return pl.ds(pl.multiple_of(cc * HD, HD), HD)

    def tall(g):
        return GROUPS[g][2] * 16

    def deep(g, zz):
        return pl.ds(pl.multiple_of(zz * 8, 8), 8), pl.ds(0, HD * GROUPS[g][2] // 4)

    def r1(g, cc):
        return remote(gp[g].at[half(cc)], cb[g], r1s, (g,), to(dc=1))

    def r2(g, d):
        n = tall(g)
        src = ysb[g].at[pl.ds(pl.multiple_of(py(d) * n, 16), n)]
        return remote(src, yb.at[g, d - 1, pl.ds(0, n)], r2s, (g, d - 1), to(dy=d))

    def r3(g, d):
        return remote(zsum.at[(g, *deep(g, pz(d)))], zb.at[(g, d - 1, *deep(g, 0))], r3s, (g, d - 1), to(dz=d))

    def r4(g):
        return remote(fin.at[(g, *deep(g, 0))], finb.at[(g, *deep(g, 0))], r4s, (g,), to(dc=1))

    def start1(g):
        go(r1(g, 1 - c))

    def start2(g):
        r1(g, 1 - c).wait_recv()
        total = (gp[g][half(c), :] + cb[g][...]).T
        ysum[g][...] = total
        ysb[g][...] = total.astype(BF16)
        for d in (1, 3, 2):
            go(r2(g, d))

    def start3(g):
        n = tall(g)
        for d in (1, 3, 2):
            r2(g, d).wait_recv()
        mine = ysum[g][pl.ds(pl.multiple_of(y * n, 8), n), :]
        term = mine + functools.reduce(jnp.add, [yb[g, d, 0:n].astype(F32) for d in range(3)])
        if GROUPS[g][2] == 4:
            zsum[g] = term
        else:
            for k in range(2 * NZ):
                zsum[g, 4 * k:4 * k + 4, 0:HD // 2] = term[4 * (k // 2):4 * (k // 2) + 4, HD // 2 * (k % 2):HD // 2 * (k % 2 + 1)]
        for d in (1, 7, 2, 6, 3, 5, 4):
            go(r3(g, d))

    def start4(g):
        for d in range(1, NZ):
            r3(g, d).wait_recv()
        term = zsum[(g, *deep(g, z))]
        for d in range(1, NZ):
            term += zb[(g, d - 1, *deep(g, 0))]
        fin[(g, *deep(g, 0))] = term
        go(r4(g))

    def finish(g):
        _, _, per, first = GROUPS[g]
        r4(g).wait_recv()
        mine, other = fin[(g, *deep(g, 0))], finb[(g, *deep(g, 0))]
        left, right = jnp.where(c == 0, mine, other), jnp.where(c == 0, other, mine)
        for h, a in enumerate((left, right)):
            a = jnp.where(c == 0, a, jnp.concatenate([a[per:], a[:per]], axis=0))
            for k in range(4 // per):
                w = HD * per // 4
                outf[first:first + per, h * HD + k * w:h * HD + (k + 1) * w] = a[4 * k:4 * k + per]

    e_forward(0, 1)
    part(0, False)
    e_send(0, 2)
    part(0, True)
    start1(0)
    e_send(1, 2)
    gw_part(0, 0)
    gw_part(0, 1)
    e_forward(1, 1)
    e_send(0, 3)
    gw_part(0, 2)
    gw_part(0, 3)
    start2(0)
    part(1, False)
    e_forward(0, 2)
    e_send(1, 3)
    e_forward(1, 2)
    part(2, False)
    part(1, True)
    start1(1)
    e_forward(0, 3)
    e_forward(1, 3)
    part(3, False)
    start2(1)
    part(2, True)
    start1(2)
    start3(0)
    for copy in loaded:
        copy.wait_send()
    part(3, True)
    start1(3)
    outs = [gw_part(2, 0)]
    start2(2)
    start2(3)
    outs.append(gw_part(2, 1))
    start3(1)
    outs.append(gw_part(2, 2))
    start3(2)
    start4(0)
    start3(3)
    outs.append(gw_part(2, 3))
    start4(1)
    finish(0)
    start4(2)
    start4(3)
    finish(1)
    finish(2)
    finish(3)
    ghs[...] = outf[0:12, :].astype(BF16)
    outs.append(pltpu.make_async_copy(ghs, gh_ref, go_sem.at[NX]))
    outs[-1].start()
    for copy in outs:
        copy.wait()
    for copy in pending:
        copy.wait_send()


def results(gw_ref, gh_ref, gw_out, gh_out, sems):
    copies = [pltpu.make_async_copy(gh_ref, gh_out, sems.at[5])]
    for i, (start, rows) in enumerate(((0, QR), (QR, QR), (2 * QR, QR), (3 * QR, 2368 - 3 * QR), (2368, VL - 2368))):
        here = pl.ds(start, rows)
        copies.append(pltpu.make_async_copy(gw_ref.at[here], gw_out.at[here], sems.at[i]))
    for copy in copies:
        copy.start()
    for copy in copies:
        copy.wait()


def local(hidden, head_weight, teacher_ids, teacher_probs, token_weight):
    hbm = pl.BlockSpec(memory_space=pl.ANY)
    dma = pltpu.SemaphoreType.DMA
    gw, gh = pl.pallas_call(
        kernel,
        grid=(1,),
        out_shape=(pltpu.VMEM((VP, DW), BF16), pltpu.VMEM((12, DW), BF16)),
        in_specs=[
            pl.BlockSpec((12, DW), lambda i: (0, 0)),
            pl.BlockSpec((16, DW), lambda i: (2368 // 16, 0)),
            hbm, hbm, hbm, hbm,
        ],
        out_specs=(hbm, hbm),
        scratch_shapes=[
            pltpu.VMEM((VP, DW), BF16),
            pltpu.VMEM((3, QR, DW), BF16),
            pltpu.VMEM((DW, 3 * QR), BF16),
            pltpu.VMEM((DW, QR), BF16),
            pltpu.VMEM((16, PW), BF16),
            pltpu.VMEM((256, 16, PW), BF16),
            pltpu.VMEM((NX, TOK, DW), BF16),
            pltpu.VMEM((NX, 2, TOK // UT, BR, UT), BF16),
            pltpu.VMEM((VP, TOK), BF16),
            pltpu.VMEM((VP, 512), BF16),
            pltpu.VMEM((VP, DW), F32),
            [pltpu.VMEM((DW, n * UT), F32) for _, n, _, _ in GROUPS],
            [pltpu.VMEM((HD, n * UT), F32) for _, n, _, _ in GROUPS],
            [pltpu.VMEM((n * UT, HD), F32) for _, n, _, _ in GROUPS],
            [pltpu.VMEM((n * UT, HD), BF16) for _, n, _, _ in GROUPS],
            pltpu.VMEM((NG, 3, 64, HD), BF16),
            pltpu.VMEM((NG, 64, HD), F32),
            pltpu.VMEM((NG, 7, 8, HD), F32),
            pltpu.VMEM((NG, 8, HD), F32),
            pltpu.VMEM((NG, 8, HD), F32),
            pltpu.VMEM((16, DW), F32),
            pltpu.VMEM((12, DW), BF16),
            pltpu.VMEM((8, TOK), F32),
            pltpu.VMEM((4 * NU, UT), F32),
            pltpu.VMEM((NX, 4 * NU, UT), F32),
            pltpu.VMEM((NC, 16, UT), F32),
            pltpu.VMEM((NZ, 16, UT), F32),
            pltpu.VMEM((NY, 16, UT), F32),
            pltpu.VMEM((2 * NX, 8, UT), F32),
            pltpu.VMEM((TOPK, TOK), jnp.int32),
            pltpu.VMEM((TOPK, TOK), F32),
            pltpu.VMEM((TOK,), F32),
            pltpu.VMEM((TOPK, TOK), jnp.int32),
            pltpu.VMEM((TOPK, TOK), F32),
            pltpu.VMEM((8, UT), F32),
            dma((4,)), dma((3,)), dma((5,)),
            dma((2, 3)), dma((2, 2, 3)), dma((2, 3)), dma((2, 2, 4)), dma((2, 2, 4)), dma((2, 3)), dma((2, 8)),
            dma((2, 4)), dma((2, 2, 2, NG)), dma((2, 2, NG)), dma((2, 3)), dma((2, 1)), dma((2, 7)), dma((2, 3)),
            dma((2, NG)), dma((2, NG, 3)), dma((2, NG, 7)), dma((2, NG)),
        ],
        compiler_params=pltpu.CompilerParams(
            collective_id=0, has_side_effects=True, vmem_limit_bytes=58 * 2**20
        ),
        name="head_backward",
    )(hidden, head_weight, head_weight, teacher_ids.T, teacher_probs.T, token_weight)
    gw, gh = pl.pallas_call(
        results,
        out_shape=(jax.ShapeDtypeStruct((VL, DW), BF16), jax.ShapeDtypeStruct((12, DW), BF16)),
        in_specs=[hbm, hbm],
        out_specs=(hbm, hbm),
        scratch_shapes=[dma((6,))],
        compiler_params=pltpu.CompilerParams(vmem_limit_bytes=2**20),
        name="results",
    )(gw, gh)
    return gh, gw


def solution(mesh):
    return jax.shard_map(
        local,
        mesh=mesh,
        in_specs=(P("vocab", "hid"), P("vocab", "hid"), P(), P(), P()),
        out_specs=(P("vocab", "hid"), P("vocab", "hid")),
        check_vma=False,
    )
```

```python
import functools

import jax
import jax.numpy as jnp
from jax import lax
from jax.experimental import pallas as pl
from jax.experimental.pallas import tpu as pltpu
from jax.sharding import PartitionSpec as P

MESH = pl.DeviceIdType.MESH
F32, BF16 = jnp.float32, jnp.bfloat16
NX, NY, NZ, NC = 4, 4, 8, 2
TOK, TOPK, UT = 768, 64, 128
GROUPS = ((0, 2, 4, 0), (2, 2, 4, 4), (4, 1, 2, 8), (5, 1, 2, 10))
NG = len(GROUPS)
VL, QR, BR = 2374, 608, 304
VP = NX * QR
HALVES = ((0, 160), (160, 144))
DW = 1024
HD = DW // 2
PW = 768
NU = TOK // UT
NN, NT = (((1,), (0,)), ((), ())), (((1,), (1,)), ((), ()))


def dot(a, b, dims=NN):
    return lax.dot_general(a, b, dims, preferred_element_type=F32)


def remote(src, dst, sems, index, device):
    return pltpu.make_async_remote_copy(
        src_ref=src, dst_ref=dst, send_sem=sems.at[(0, *index)], recv_sem=sems.at[(1, *index)],
        device_id=device, device_id_type=MESH,
    )


def fold(a):
    return jnp.concatenate([a[:, u * UT:(u + 1) * UT] for u in range(NU)], axis=0)


def pieces(a):
    first = a.astype(BF16)
    rest = a - first.astype(F32)
    second = rest.astype(BF16)
    return first, second, (rest - second.astype(F32)).astype(BF16)


def kernel(
    hid_ref, edge_ref, w_ref, ids_ref, probs_ref, tw_ref, gw_ref, gh_ref,
    wv, wq, wta, wtb, pack, hp, hc, ex, tgt, st, gw, gp, cb, ysum, ysb, yb, zsum, zb, fin, finb, outf, ghs,
    psend, precv, sraw, sown, sx, scr, sz, sy, fac, idr, prr, twr, idp, wpp, vec,
    wl_sem, hl_sem, go_sem, xs, ws, ps, ays, azs, bzs, bys, acs, bcs, es, fs, sxs, scs, szs, sys_, r1s, r2s, r3s, r4s,
):
    v = lax.axis_index("vocab")
    x = lax.axis_index("hid")
    y, z, c = v // (NZ * NC), lax.rem(v // NC, NZ), lax.rem(v, NC)

    def px(d):
        return lax.rem(x + d + NX, NX)

    slots = (0, -1, 1, 2)

    def py(d):
        return lax.rem(y + d + NY, NY)

    def pz(d):
        return lax.rem(z + d + NZ, NZ)

    def to(dx=0, dy=0, dz=0, dc=0):
        return ((py(dy) * NZ + pz(dz)) * NC + lax.rem(c + dc, NC), px(dx))

    pending = []

    def go(copy):
        copy.start()
        pending.append(copy)

    loads = []
    for k in range(NX):
        rows = QR if k < NX - 1 else 2368 - 3 * QR
        loads.append(pltpu.make_async_copy(w_ref.at[pl.ds(k * QR, rows)], wv.at[pl.ds(k * QR, rows)], wl_sem.at[k]))
    smalls = [
        pltpu.make_async_copy(src, dst, hl_sem.at[i])
        for i, (src, dst) in enumerate(((ids_ref, idr), (probs_ref, prr), (tw_ref, twr)))
    ]
    for copy in loads + smalls:
        copy.start()

    def place_a(cc, zz, yy):
        return ((cc * NZ + zz) * NY + yy) * 2

    def place_b(cc, yy, zz):
        return 128 + ((cc * NY + yy) * NZ + zz) * 2

    def place(q):
        return jnp.where(q < 2, place_a(c, z, y), place_b(c, y, z)) + lax.rem(q, 2)

    pack[0:12, :] = hid_ref[:, 0:PW]
    for h in range(3):
        pack[12:16, 256 * h:256 * h + 256] = hid_ref[4 * h:4 * h + 4, PW:DW]
    hp[place(x)] = pack[...]
    edge = lax.broadcasted_iota(jnp.int32, (16, DW), 0) < VL - 2368
    wv[pl.ds(2368, 16), :] = jnp.where(edge, edge_ref[...], jnp.zeros((16, DW), BF16))
    wv[pl.ds(2384, 48), :] = jnp.zeros((48, DW), BF16)

    peers = [dict(dx=d) for d in (1, 2, 3)] + [dict(dy=d) for d in (1, 2, 3)]
    peers += [dict(dz=d) for d in range(1, NZ)] + [dict(dc=1)]
    barrier = pltpu.get_barrier_semaphore()
    for peer in peers:
        pl.semaphore_signal(barrier, inc=1, device_id=to(**peer), device_id_type=MESH)
    pl.semaphore_wait(barrier, len(peers))

    for d in (1, 2, 3):
        go(remote(pack, hp.at[place(x)], xs, (d - 1,), to(dx=d)))
    for copy in loads:
        copy.wait()

    def w_copy(d):
        src = wv.at[pl.ds(pl.multiple_of(px(d) * QR, 16), BR)]
        return remote(src, wq.at[d - 1, pl.ds(0, BR)], ws, (0, d - 1), to(dx=d))

    ways = ((1, 2, 0), (-1, 2, 1), (-1, -1, 0), (1, 1, 1))

    def h_at(j):
        way, _, part = ways[j]
        first, n = HALVES[part]
        return wq.at[0 if way == 1 else 2, pl.ds(BR + first, n)]

    def h_copy(j):
        way, quarter, part = ways[j]
        first, n = HALVES[part]
        src = wv.at[pl.ds(pl.multiple_of(px(quarter) * QR + BR + first, 16), n)]
        return remote(src, h_at(j), ws, (1, j), to(dx=way))

    for d in (1, 3, 2):
        go(w_copy(d))
    for j in range(4):
        go(h_copy(j))
    loaded = [pending.pop() for _ in range(7)]

    for copy in smalls:
        copy.wait()
    row = lax.broadcasted_iota(jnp.int32, (TOK, TOK), 0)
    col = lax.broadcasted_iota(jnp.int32, (TOK, TOK), 1)
    source = jnp.zeros((TOK, TOK), jnp.int32)
    for unit, units, per, first in GROUPS:
        i = col - unit * UT
        here = (i >= 0) & (i < units * UT)
        source = jnp.where(here, (i // per) * 12 + first + lax.rem(i, per), source)
    perm = jnp.where(row == source, 1.0, 0.0).astype(BF16)
    near = idr[...] - v * VL
    near = jnp.where((near >= 0) & (near < VL), near, 4095)
    low, high = (near & 255).astype(F32).astype(BF16), (near >> 8).astype(F32).astype(BF16)
    idp[...] = (dot(high, perm) * 256.0 + dot(low, perm)).astype(jnp.int32)
    probs = functools.reduce(jnp.add, [dot(a, perm) for a in pieces(prr[...])])
    tw = functools.reduce(jnp.add, [dot(a, perm) for a in pieces(twr[...].reshape(1, TOK))])
    wpp[...] = probs * tw
    vec[0:NU, :] = fold(tw * jnp.sum(probs, axis=0, keepdims=True))

    def target(lo, hi):
        @pl.loop(lo, hi)
        def _(i):
            rows = pl.ds(pl.multiple_of((i // 6) * BR, 16), BR)
            lanes = pl.ds(pl.multiple_of(lax.rem(i, 6) * 128, 128), 128)
            index = lax.broadcasted_iota(jnp.int16, (BR, 128), 0)
            total = jnp.zeros((BR, 128), BF16)
            for k in range(TOPK):
                here = (idp[pl.ds(k, 1), lanes] - (i // 6) * BR).astype(jnp.int16)
                mass = wpp[pl.ds(k, 1), lanes].astype(BF16)
                total = jnp.where(
                    jnp.broadcast_to(here, (BR, 128)) == index, jnp.broadcast_to(mass, (BR, 128)), total
                )
            tgt[rows, lanes] = total

    for d in (1, 2, 3):
        at = hp.at[place(px(-d))]
        remote(at, at, xs, (d - 1,), to(dx=d)).wait_recv()

    def block(start, size):
        return hp.at[pl.ds(start, size)]

    def ay(dd, d):
        at = block(place_a(c, z, py(dd)), 2)
        return remote(at, at, ays, (d - 1,), to(dy=d))

    def az(origin, way, s):
        at = block(place_a(c, pz(origin), 0), 8)
        return remote(at, at, azs, (way, s - 1), to(dz=1 if way == 0 else -1))

    def bz(origin, way, s):
        at = block(place_b(c, y, pz(origin)), 2)
        return remote(at, at, bzs, (way, s - 1), to(dz=1 if way == 0 else -1))

    def by(dd, d):
        at = block(place_b(c, py(dd), 0), 16)
        return remote(at, at, bys, (d - 1,), to(dy=d))

    def ac(k, cc):
        at = block(place_a(cc, pz(k), 0), 8)
        return remote(at, at, acs, (k,), to(dc=1))

    def bc(k, cc):
        at = block(place_b(cc, py(k), 0), 16)
        return remote(at, at, bcs, (k,), to(dc=1))

    def ring(make, s, cross=None):
        for way, sign, steps in ((0, -1, 4), (1, 1, 3)):
            if s <= steps:
                make(sign * s, way, s).wait_recv()
                if s < steps:
                    go(make(sign * s, way, s + 1))
                if cross is not None:
                    go(cross((sign * s) % NZ, c))

    for d in (1, 3, 2):
        go(ay(0, d))
    go(bz(0, 0, 1))
    go(bz(0, 1, 1))
    target(0, 5)
    ring(bz, 1)
    for d in (1, 2, 3):
        ay(-d, d).wait_recv()
    go(az(0, 0, 1))
    go(az(0, 1, 1))
    go(ac(0, c))
    target(5, 10)
    ring(bz, 2)
    target(10, 15)
    ring(bz, 3)
    ring(az, 1, ac)
    target(15, 20)
    ring(bz, 4)
    for d in (1, 3, 2):
        go(by(0, d))
    go(bc(0, c))
    target(20, 27)
    ring(az, 2, ac)
    target(27, 37)
    ring(az, 3, ac)
    target(37, 48)
    ring(az, 4, ac)
    for d in (1, 3, 2):
        by(-d, d).wait_recv()
        go(bc((-d) % NY, c))
    for k in range(NZ):
        ac(k, 1 - c).wait_recv()
    for k in range(NY):
        bc(k, 1 - c).wait_recv()

    kinds = [(per, first) for _, _, per, first in GROUPS]
    kinds += [(per, 12 + first % 4) for _, _, per, first in GROUPS]
    height = sum(16 * per for per, _ in kinds)
    row = lax.broadcasted_iota(jnp.int32, (height, 256), 0)
    col = lax.broadcasted_iota(jnp.int32, (height, 256), 1)
    pick = jnp.zeros((height, 256), jnp.int32)
    begins, start = [], 0
    for per, first in kinds:
        i = row - start
        here = (i >= 0) & (i < 16 * per)
        zz, rest = i // (2 * per), lax.rem(i, 2 * per)
        pick = jnp.where(here, (rest // per) * 128 + zz * 16 + first + lax.rem(rest, per), pick)
        begins.append(start)
        start += 16 * per
    perm = jnp.where(col == pick, 1.0, 0.0).astype(BF16)

    def unpack(k, yy):
        q = px(k)
        parts = []
        for cc in range(NC):
            for zz in range(NZ):
                at = jnp.where(q < 2, place_a(cc, zz, yy), place_b(cc, yy, zz)) + lax.rem(q, 2)
                parts.append(hp[at])
        rows = dot(perm, jnp.concatenate(parts, axis=0)).astype(BF16)
        for g, (unit, _, per, first) in enumerate(GROUPS):
            n, h = 16 * per, 256 * (first // 4)
            here = pl.ds(pl.multiple_of(unit * UT + yy * n, 16), n)
            hc[q, here, 0:PW] = rows[begins[g]:begins[g] + n]
            hc[q, here, PW:DW] = rows[begins[NG + g]:begins[NG + g] + n, h:h + 256]

    @pl.loop(0, 3 * NY)
    def _(i):
        unpack(i // NY - 1, lax.rem(i, NY))

    def two(quarter, part, slot, i):
        first, n = HALVES[part]
        toks = slice(256 * i, 256 * i + 256)
        rows = pl.ds(pl.multiple_of(px(quarter) * QR + BR + first, 16), n)
        other = hc[px(-1 if slot == 0 else 1), toks, :]
        return dot(wv[rows, :], hc[x, toks, :], NT) + dot(wq[slot, BR + first:BR + first + n, :], other, NT)

    def p_copy(part, i):
        first, n = HALVES[part]
        here = pl.ds(first, n)
        return remote(psend.at[i, here], precv.at[i, here], ps, (part, i), to(dx=(1, -1)[part]))

    def h_wait(j):
        remote(h_at(j), h_at(j), ws, (1, j), to(dx=ways[j][0])).wait_recv()

    for part_ in range(2):
        h_wait(part_)
        for i in range(TOK // 256):
            first, n = HALVES[part_]
            psend[i, first:first + n, :] = two((1, -1)[part_], part_, (0, 2)[part_], i)
            go(p_copy(part_, i))

    @pl.loop(0, NY)
    def _(i):
        unpack(2, i)

    def numerators(b, i, total):
        toks = pl.ds(pl.multiple_of(i * 256, 256), 256)
        real = lax.broadcasted_iota(jnp.int32, (BR, 256), 0) + (x * QR + b * BR) < VL
        total = jnp.where(real, total, -1e30)
        top = jnp.max(total, axis=0, keepdims=True)
        shifted = jnp.exp(total - top)
        sraw[pl.ds(b, 1), toks] = top
        sraw[pl.ds(2 + b, 1), toks] = jnp.sum(shifted, axis=0, keepdims=True)
        shifted = shifted.astype(BF16)
        ex[x, b, 2 * i] = shifted[:, 0:128]
        ex[x, b, 2 * i + 1] = shifted[:, 128:256]

    def e_at(q, b, g):
        return ex.at[q, b, pl.ds(GROUPS[g][0], GROUPS[g][1])]

    def e_copy(q, b, g, way):
        at = e_at(q, b, g)
        return remote(at, at, es, (way, b, g), to(dx=1 if way == 0 else -1))

    def f_copy(q, b, g):
        at = e_at(q, b, g)
        return remote(at, at, fs, (b, g), to(dx=1 if b == 0 else -1))

    def e_send(b, g):
        go(e_copy(x, b, g, 0))
        go(e_copy(x, b, g, 1))

    def e_wait(b, g, way):
        e_copy(px(-1 if way == 0 else 1), b, g, way).wait_recv()

    def e_forward(b, g):
        e_wait(b, g, b)
        go(f_copy(px(-1 if b == 0 else 1), b, g))

    for d in (1, 2, 3):
        at = wq.at[d - 1, pl.ds(0, BR)]
        remote(at, at, ws, (0, d - 1), to(dx=d)).wait_recv()

    @pl.loop(0, TOK // 256)
    def _(i):
        toks = pl.ds(pl.multiple_of(i * 256, 256), 256)
        total = dot(wv[pl.ds(pl.multiple_of(x * QR, 16), BR), :], hc[x, toks, :], NT)
        for d in (1, 2, 3):
            total += dot(wq[d - 1, 0:BR, :], hc[px(-d), toks, :], NT)
        numerators(0, i, total)

    h_wait(2)
    h_wait(3)
    for i in range(TOK // 256):
        for part_ in range(2):
            first, n = HALVES[part_]
            gw[i * BR + first:i * BR + first + n, 0:256] = two(0, part_, (2, 0)[part_], i)
    for i in range(0, 3 * QR, 128):
        pieces_, j = [], i
        while j < min(i + 128, 3 * QR):
            k = j // QR
            n = min(i + 128, 3 * QR, (k + 1) * QR) - j
            pieces_.append(wv[pl.ds(pl.multiple_of(px(slots[k]) * QR + j - k * QR, 16), n), :])
            j += n
        wta[:, i:j] = jnp.concatenate(pieces_, axis=0).T
    for i in range(0, QR, 128):
        n = min(128, QR - i)
        wtb[:, i:i + n] = wv[pl.ds(pl.multiple_of(px(2) * QR + i, 16), n), :].T

    for i in range(TOK // 256):
        for part_ in range(2):
            p_copy(part_, i).wait_recv()
    e_send(0, 0)

    @pl.loop(0, TOK // 256)
    def _(i):
        numerators(1, i, gw[pl.ds(pl.multiple_of(i * BR, 8), BR), 0:256] + precv[i])


    def sx_copy(q, d):
        return remote(sown, sx.at[q], sxs, (d - 1,), to(dx=d))

    for j in range(4):
        sown[j * NU:(j + 1) * NU, :] = fold(sraw[pl.ds(j, 1), :])
    for d in (1, 3, 2):
        go(sx_copy(x, d))
    e_send(1, 0)
    sx[x] = sown[...]
    for d in (1, 3, 2):
        sx_copy(px(-d), d).wait_recv()
    tops = [sx[q, b * NU:(b + 1) * NU, :] for q in range(NX) for b in range(2)]
    sums = [sx[q, (2 + b) * NU:(3 + b) * NU, :] for q in range(NX) for b in range(2)]

    def merge(tops, sums):
        top = functools.reduce(jnp.maximum, tops)
        return top, functools.reduce(jnp.add, [s * jnp.exp(t - top) for s, t in zip(sums, tops)])

    def spread(buf, sems, me, top, total, moves, slot, between):
        buf[me] = jnp.zeros((16, UT), F32)
        buf[me, 0:NU, :] = top
        buf[me, NU:2 * NU, :] = total
        for i, move in enumerate(moves):
            go(remote(buf.at[me], buf.at[me], sems, (i,), to(**move)))
        between()
        for i, move in enumerate(moves):
            at = buf.at[slot(move)]
            remote(at, at, sems, (i,), to(**move)).wait_recv()
        n = len(moves) + 1
        return merge([buf[k, 0:NU, :] for k in range(n)], [buf[k, NU:2 * NU, :] for k in range(n)])

    e_forward(0, 0)
    top, total = merge(tops, sums)
    top, total = spread(scr, scs, c, top, total, [dict(dc=1)], lambda m: 1 - c, lambda: None)

    def between_z():
        e_forward(1, 0)
        e_send(0, 1)

    def between_y():
        e_send(1, 1)

    moves = [dict(dz=d) for d in (4, 3, 5, 2, 6, 1, 7)]
    top, total = spread(sz, szs, z, top, total, moves, lambda m: pz(-m["dz"]), between_z)
    moves = [dict(dy=d) for d in (2, 1, 3)]
    top, total = spread(sy, sys_, y, top, total, moves, lambda m: py(-m["dy"]), between_y)
    scale = vec[0:NU, :] / total
    for i in range(2 * NX):
        fac[i, 0:NU, :] = scale * jnp.exp(tops[i] - top)

    def part(g, far):
        unit, units, _, _ = GROUPS[g]
        size, lane = units * UT, (256, 0, 256, 384)[g]
        for k in (3,) if far else (0, 1, 2):
            q = px(slots[k])
            if k == 3:
                f_copy(q, 0, g).wait_recv()
                f_copy(q, 1, g).wait_recv()
            elif k != 0:
                e_wait(2 - k, g, k - 1)
            for b in range(2):
                rows = pl.ds(pl.multiple_of(q * QR + b * BR, 16), BR)
                for u in range(units):
                    toks = pl.ds((unit + u) * UT, UT)
                    e = ex[q, b, unit + u].astype(F32)
                    score = fac[2 * q + b, pl.ds(unit + u, 1), :] * e - tgt[rows, toks].astype(F32)
                    here = k * QR + b * BR
                    st[here:here + BR, lane + u * UT:lane + (u + 1) * UT] = score.astype(BF16)

        @pl.loop(0, 2)
        def _(i):
            at = pl.ds(pl.multiple_of(i * HD, HD), HD)
            if far:
                gp[g][at, :] += dot(wtb[at, :], st[3 * QR:VP, lane:lane + size])
            else:
                gp[g][at, :] = dot(wta[at, :], st[0:3 * QR, lane:lane + size])

    def gw_part(g, k):
        rows = slice(k * QR, (k + 1) * QR)
        if g == 0:
            gw[rows, :] = dot(st[rows, 256:512], hc[x, 0:256, :])
        else:
            term = dot(st[rows, :], hc[x, 256:TOK, :])
            wv[rows, :] = (gw[rows, :] + term).astype(BF16)
            there = pl.ds(pl.multiple_of(px(slots[k]) * QR, 16), QR)
            copy = pltpu.make_async_copy(wv.at[pl.ds(k * QR, QR)], gw_ref.at[there], go_sem.at[k])
            copy.start()
            return copy

    def half(cc):
        return pl.ds(pl.multiple_of(cc * HD, HD), HD)

    def tall(g):
        return GROUPS[g][2] * 16

    def deep(g, zz):
        return pl.ds(pl.multiple_of(zz * 8, 8), 8), pl.ds(0, HD * GROUPS[g][2] // 4)

    def r1(g, cc):
        return remote(gp[g].at[half(cc)], cb[g], r1s, (g,), to(dc=1))

    def r2(g, d):
        n = tall(g)
        src = ysb[g].at[pl.ds(pl.multiple_of(py(d) * n, 16), n)]
        return remote(src, yb.at[g, d - 1, pl.ds(0, n)], r2s, (g, d - 1), to(dy=d))

    def r3(g, d):
        return remote(zsum.at[(g, *deep(g, pz(d)))], zb.at[(g, d - 1, *deep(g, 0))], r3s, (g, d - 1), to(dz=d))

    def r4(g):
        return remote(fin.at[(g, *deep(g, 0))], finb.at[(g, *deep(g, 0))], r4s, (g,), to(dc=1))

    def start1(g):
        go(r1(g, 1 - c))

    def start2(g):
        r1(g, 1 - c).wait_recv()
        total = (gp[g][half(c), :] + cb[g][...]).T
        ysum[g][...] = total
        ysb[g][...] = total.astype(BF16)
        for d in (1, 3, 2):
            go(r2(g, d))

    def start3(g):
        n = tall(g)
        for d in (1, 3, 2):
            r2(g, d).wait_recv()
        mine = ysum[g][pl.ds(pl.multiple_of(y * n, 8), n), :]
        term = mine + functools.reduce(jnp.add, [yb[g, d, 0:n].astype(F32) for d in range(3)])
        if GROUPS[g][2] == 4:
            zsum[g] = term
        else:
            for k in range(2 * NZ):
                zsum[g, 4 * k:4 * k + 4, 0:HD // 2] = term[4 * (k // 2):4 * (k // 2) + 4, HD // 2 * (k % 2):HD // 2 * (k % 2 + 1)]
        for d in (1, 7, 2, 6, 3, 5, 4):
            go(r3(g, d))

    def start4(g):
        for d in range(1, NZ):
            r3(g, d).wait_recv()
        term = zsum[(g, *deep(g, z))]
        for d in range(1, NZ):
            term += zb[(g, d - 1, *deep(g, 0))]
        fin[(g, *deep(g, 0))] = term
        go(r4(g))

    def finish(g):
        _, _, per, first = GROUPS[g]
        r4(g).wait_recv()
        mine, other = fin[(g, *deep(g, 0))], finb[(g, *deep(g, 0))]
        left, right = jnp.where(c == 0, mine, other), jnp.where(c == 0, other, mine)
        for h, a in enumerate((left, right)):
            a = jnp.where(c == 0, a, jnp.concatenate([a[per:], a[:per]], axis=0))
            for k in range(4 // per):
                w = HD * per // 4
                outf[first:first + per, h * HD + k * w:h * HD + (k + 1) * w] = a[4 * k:4 * k + per]

    e_forward(0, 1)
    part(0, False)
    e_send(0, 2)
    part(0, True)
    start1(0)
    e_send(1, 2)
    gw_part(0, 0)
    gw_part(0, 1)
    e_forward(1, 1)
    e_send(0, 3)
    gw_part(0, 2)
    gw_part(0, 3)
    start2(0)
    e_send(1, 3)
    part(1, False)
    e_forward(0, 2)
    e_forward(1, 2)
    part(2, False)
    part(1, True)
    start1(1)
    e_forward(0, 3)
    e_forward(1, 3)
    start2(1)
    part(3, False)
    part(2, True)
    start1(2)
    start3(0)
    for copy in loaded:
        copy.wait_send()
    part(3, True)
    start1(3)
    start2(2)
    start3(1)
    outs = [gw_part(2, 0)]
    start2(3)
    start4(0)
    outs.append(gw_part(2, 1))
    start3(2)
    outs.append(gw_part(2, 2))
    start3(3)
    start4(1)
    outs.append(gw_part(2, 3))
    finish(0)
    start4(2)
    start4(3)
    finish(1)
    finish(2)
    finish(3)
    ghs[...] = outf[0:12, :].astype(BF16)
    outs.append(pltpu.make_async_copy(ghs, gh_ref, go_sem.at[NX]))
    outs[-1].start()
    for copy in outs:
        copy.wait()
    for copy in pending:
        copy.wait_send()


def results(gw_ref, gh_ref, gw_out, gh_out, sems):
    copies = [pltpu.make_async_copy(gh_ref, gh_out, sems.at[5])]
    for i, (start, rows) in enumerate(((0, QR), (QR, QR), (2 * QR, QR), (3 * QR, 2368 - 3 * QR), (2368, VL - 2368))):
        here = pl.ds(start, rows)
        copies.append(pltpu.make_async_copy(gw_ref.at[here], gw_out.at[here], sems.at[i]))
    for copy in copies:
        copy.start()
    for copy in copies:
        copy.wait()


def local(hidden, head_weight, teacher_ids, teacher_probs, token_weight):
    hbm = pl.BlockSpec(memory_space=pl.ANY)
    dma = pltpu.SemaphoreType.DMA
    gw, gh = pl.pallas_call(
        kernel,
        grid=(1,),
        out_shape=(pltpu.VMEM((VP, DW), BF16), pltpu.VMEM((12, DW), BF16)),
        in_specs=[
            pl.BlockSpec((12, DW), lambda i: (0, 0)),
            pl.BlockSpec((16, DW), lambda i: (2368 // 16, 0)),
            hbm, hbm, hbm, hbm,
        ],
        out_specs=(hbm, hbm),
        scratch_shapes=[
            pltpu.VMEM((VP, DW), BF16),
            pltpu.VMEM((3, QR, DW), BF16),
            pltpu.VMEM((DW, 3 * QR), BF16),
            pltpu.VMEM((DW, QR), BF16),
            pltpu.VMEM((16, PW), BF16),
            pltpu.VMEM((256, 16, PW), BF16),
            pltpu.VMEM((NX, TOK, DW), BF16),
            pltpu.VMEM((NX, 2, TOK // UT, BR, UT), BF16),
            pltpu.VMEM((VP, TOK), BF16),
            pltpu.VMEM((VP, 512), BF16),
            pltpu.VMEM((VP, DW), F32),
            [pltpu.VMEM((DW, n * UT), F32) for _, n, _, _ in GROUPS],
            [pltpu.VMEM((HD, n * UT), F32) for _, n, _, _ in GROUPS],
            [pltpu.VMEM((n * UT, HD), F32) for _, n, _, _ in GROUPS],
            [pltpu.VMEM((n * UT, HD), BF16) for _, n, _, _ in GROUPS],
            pltpu.VMEM((NG, 3, 64, HD), BF16),
            pltpu.VMEM((NG, 64, HD), F32),
            pltpu.VMEM((NG, 7, 8, HD), F32),
            pltpu.VMEM((NG, 8, HD), F32),
            pltpu.VMEM((NG, 8, HD), F32),
            pltpu.VMEM((16, DW), F32),
            pltpu.VMEM((12, DW), BF16),
            pltpu.VMEM((TOK // 256, BR, 256), F32),
            pltpu.VMEM((TOK // 256, BR, 256), F32),
            pltpu.VMEM((8, TOK), F32),
            pltpu.VMEM((4 * NU, UT), F32),
            pltpu.VMEM((NX, 4 * NU, UT), F32),
            pltpu.VMEM((NC, 16, UT), F32),
            pltpu.VMEM((NZ, 16, UT), F32),
            pltpu.VMEM((NY, 16, UT), F32),
            pltpu.VMEM((2 * NX, 8, UT), F32),
            pltpu.VMEM((TOPK, TOK), jnp.int32),
            pltpu.VMEM((TOPK, TOK), F32),
            pltpu.VMEM((TOK,), F32),
            pltpu.VMEM((TOPK, TOK), jnp.int32),
            pltpu.VMEM((TOPK, TOK), F32),
            pltpu.VMEM((8, UT), F32),
            dma((4,)), dma((3,)), dma((5,)),
            dma((2, 3)), dma((2, 2, 4)), dma((2, 2, 3)), dma((2, 3)), dma((2, 2, 4)), dma((2, 2, 4)), dma((2, 3)), dma((2, 8)),
            dma((2, 4)), dma((2, 2, 2, NG)), dma((2, 2, NG)), dma((2, 3)), dma((2, 1)), dma((2, 7)), dma((2, 3)),
            dma((2, NG)), dma((2, NG, 3)), dma((2, NG, 7)), dma((2, NG)),
        ],
        compiler_params=pltpu.CompilerParams(
            collective_id=0, has_side_effects=True, vmem_limit_bytes=117 * 2**19
        ),
        name="head_backward",
    )(hidden, head_weight, head_weight, teacher_ids.T, teacher_probs.T, token_weight)
    gw, gh = pl.pallas_call(
        results,
        out_shape=(jax.ShapeDtypeStruct((VL, DW), BF16), jax.ShapeDtypeStruct((12, DW), BF16)),
        in_specs=[hbm, hbm],
        out_specs=(hbm, hbm),
        scratch_shapes=[dma((6,))],
        compiler_params=pltpu.CompilerParams(vmem_limit_bytes=2**20),
        name="results",
    )(gw, gh)
    return gh, gw


def solution(mesh):
    return jax.shard_map(
        local,
        mesh=mesh,
        in_specs=(P("vocab", "hid"), P("vocab", "hid"), P(), P(), P()),
        out_specs=(P("vocab", "hid"), P("vocab", "hid")),
        check_vma=False,
    )
```

```python
import functools

import jax
import jax.numpy as jnp
from jax import lax
from jax.experimental import pallas as pl
from jax.experimental.pallas import tpu as pltpu
from jax.sharding import PartitionSpec as P

MESH = pl.DeviceIdType.MESH
F32, BF16 = jnp.float32, jnp.bfloat16
NX, NY, NZ, NC = 4, 4, 8, 2
TOK, TOPK, UT = 768, 64, 128
GROUPS = ((0, 2, 4, 0), (2, 2, 4, 4), (4, 1, 2, 8), (5, 1, 2, 10))
NG = len(GROUPS)
VL, QR, BR = 2374, 608, 304
VP = NX * QR
HALVES = ((0, 160), (160, 144))
DW = 1024
HD = DW // 2
PW = 768
NU = TOK // UT
NN, NT = (((1,), (0,)), ((), ())), (((1,), (1,)), ((), ()))


def dot(a, b, dims=NN):
    return lax.dot_general(a, b, dims, preferred_element_type=F32)


def remote(src, dst, sems, index, device):
    return pltpu.make_async_remote_copy(
        src_ref=src, dst_ref=dst, send_sem=sems.at[(0, *index)], recv_sem=sems.at[(1, *index)],
        device_id=device, device_id_type=MESH,
    )


def fold(a):
    return jnp.concatenate([a[:, u * UT:(u + 1) * UT] for u in range(NU)], axis=0)


def pieces(a):
    first = a.astype(BF16)
    rest = a - first.astype(F32)
    second = rest.astype(BF16)
    return first, second, (rest - second.astype(F32)).astype(BF16)


def kernel(
    hid_ref, edge_ref, w_ref, ids_ref, probs_ref, tw_ref, gw_ref, gh_ref,
    wv, wq, wta, wtb, pack, hp, hc, ex, tgt, st, gw, gp, gt, cb, ysb, yb, zsum, zb, outf, ghs,
    psend, precv, sraw, sown, sx, scr, sz, sy, fac, idr, prr, twr, idp, wpp, vec,
    wl_sem, hl_sem, go_sem, xs, ws, ps, ays, azs, bzs, bys, acs, bcs, es, fs, sxs, scs, szs, sys_, r1s, r2s, r3s,
):
    v = lax.axis_index("vocab")
    x = lax.axis_index("hid")
    y, z, c = v // (NZ * NC), lax.rem(v // NC, NZ), lax.rem(v, NC)

    def px(d):
        return lax.rem(x + d + NX, NX)

    slots = (0, -1, 1, 2)

    def py(d):
        return lax.rem(y + d + NY, NY)

    def pz(d):
        return lax.rem(z + d + NZ, NZ)

    def to(dx=0, dy=0, dz=0, dc=0):
        return ((py(dy) * NZ + pz(dz)) * NC + lax.rem(c + dc, NC), px(dx))

    pending = []

    def go(copy):
        copy.start()
        pending.append(copy)

    loads = []
    for k in range(NX):
        rows = QR if k < NX - 1 else 2368 - 3 * QR
        loads.append(pltpu.make_async_copy(w_ref.at[pl.ds(k * QR, rows)], wv.at[pl.ds(k * QR, rows)], wl_sem.at[k]))
    smalls = [
        pltpu.make_async_copy(src, dst, hl_sem.at[i])
        for i, (src, dst) in enumerate(((ids_ref, idr), (probs_ref, prr), (tw_ref, twr)))
    ]
    for copy in loads + smalls:
        copy.start()

    def place_a(cc, zz, yy):
        return ((cc * NZ + zz) * NY + yy) * 2

    def place_b(cc, yy, zz):
        return 128 + ((cc * NY + yy) * NZ + zz) * 2

    def place(q):
        return jnp.where(q < 2, place_a(c, z, y), place_b(c, y, z)) + lax.rem(q, 2)

    pack[0:12, :] = hid_ref[:, 0:PW]
    for h in range(3):
        pack[12:16, 256 * h:256 * h + 256] = hid_ref[4 * h:4 * h + 4, PW:DW]
    hp[place(x)] = pack[...]
    edge = lax.broadcasted_iota(jnp.int32, (16, DW), 0) < VL - 2368
    wv[pl.ds(2368, 16), :] = jnp.where(edge, edge_ref[...], jnp.zeros((16, DW), BF16))
    wv[pl.ds(2384, 48), :] = jnp.zeros((48, DW), BF16)

    peers = [dict(dx=d) for d in (1, 2, 3)] + [dict(dy=d) for d in (1, 2, 3)]
    peers += [dict(dz=d) for d in range(1, NZ)] + [dict(dc=1)]
    barrier = pltpu.get_barrier_semaphore()
    for peer in peers:
        pl.semaphore_signal(barrier, inc=1, device_id=to(**peer), device_id_type=MESH)
    pl.semaphore_wait(barrier, len(peers))

    for d in (1, 2, 3):
        go(remote(pack, hp.at[place(x)], xs, (d - 1,), to(dx=d)))
    for copy in loads:
        copy.wait()

    def w_copy(d):
        src = wv.at[pl.ds(pl.multiple_of(px(d) * QR, 16), BR)]
        return remote(src, wq.at[d - 1, pl.ds(0, BR)], ws, (0, d - 1), to(dx=d))

    ways = ((1, 2, 0), (-1, 2, 1), (-1, -1, 0), (1, 1, 1))

    def h_at(j):
        way, _, part = ways[j]
        first, n = HALVES[part]
        return wq.at[0 if way == 1 else 2, pl.ds(BR + first, n)]

    def h_copy(j):
        way, quarter, part = ways[j]
        first, n = HALVES[part]
        src = wv.at[pl.ds(pl.multiple_of(px(quarter) * QR + BR + first, 16), n)]
        return remote(src, h_at(j), ws, (1, j), to(dx=way))

    for d in (1, 3, 2):
        go(w_copy(d))
    for j in range(4):
        go(h_copy(j))
    loaded = [pending.pop() for _ in range(7)]

    for copy in smalls:
        copy.wait()
    row = lax.broadcasted_iota(jnp.int32, (TOK, TOK), 0)
    col = lax.broadcasted_iota(jnp.int32, (TOK, TOK), 1)
    source = jnp.zeros((TOK, TOK), jnp.int32)
    for unit, units, per, first in GROUPS:
        i = col - unit * UT
        here = (i >= 0) & (i < units * UT)
        chip, core = lax.rem(i // per, NY * NZ), i // (per * NY * NZ)
        source = jnp.where(here, (chip * NC + core) * 12 + first + lax.rem(i, per), source)
    perm = jnp.where(row == source, 1.0, 0.0).astype(BF16)
    near = idr[...] - v * VL
    near = jnp.where((near >= 0) & (near < VL), near, 4095)
    low, high = (near & 255).astype(F32).astype(BF16), (near >> 8).astype(F32).astype(BF16)
    idp[...] = (dot(high, perm) * 256.0 + dot(low, perm)).astype(jnp.int32)
    probs = functools.reduce(jnp.add, [dot(a, perm) for a in pieces(prr[...])])
    tw = functools.reduce(jnp.add, [dot(a, perm) for a in pieces(twr[...].reshape(1, TOK))])
    wpp[...] = probs * tw
    vec[0:NU, :] = fold(tw * jnp.sum(probs, axis=0, keepdims=True))

    def target(lo, hi):
        @pl.loop(lo, hi)
        def _(i):
            rows = pl.ds(pl.multiple_of((i // 6) * BR, 16), BR)
            lanes = pl.ds(pl.multiple_of(lax.rem(i, 6) * 128, 128), 128)
            index = lax.broadcasted_iota(jnp.int16, (BR, 128), 0)
            total = jnp.zeros((BR, 128), BF16)
            for k in range(TOPK):
                here = (idp[pl.ds(k, 1), lanes] - (i // 6) * BR).astype(jnp.int16)
                mass = wpp[pl.ds(k, 1), lanes].astype(BF16)
                total = jnp.where(
                    jnp.broadcast_to(here, (BR, 128)) == index, jnp.broadcast_to(mass, (BR, 128)), total
                )
            tgt[rows, lanes] = total

    for d in (1, 2, 3):
        at = hp.at[place(px(-d))]
        remote(at, at, xs, (d - 1,), to(dx=d)).wait_recv()

    def block(start, size):
        return hp.at[pl.ds(start, size)]

    def ay(dd, d):
        at = block(place_a(c, z, py(dd)), 2)
        return remote(at, at, ays, (d - 1,), to(dy=d))

    def az(origin, way, s):
        at = block(place_a(c, pz(origin), 0), 8)
        return remote(at, at, azs, (way, s - 1), to(dz=1 if way == 0 else -1))

    def bz(origin, way, s):
        at = block(place_b(c, y, pz(origin)), 2)
        return remote(at, at, bzs, (way, s - 1), to(dz=1 if way == 0 else -1))

    def by(dd, d):
        at = block(place_b(c, py(dd), 0), 16)
        return remote(at, at, bys, (d - 1,), to(dy=d))

    def ac(k, cc):
        at = block(place_a(cc, pz(k), 0), 8)
        return remote(at, at, acs, (k,), to(dc=1))

    def bc(k, cc):
        at = block(place_b(cc, py(k), 0), 16)
        return remote(at, at, bcs, (k,), to(dc=1))

    def ring(make, s, cross=None):
        for way, sign, steps in ((0, -1, 4), (1, 1, 3)):
            if s <= steps:
                make(sign * s, way, s).wait_recv()
                if s < steps:
                    go(make(sign * s, way, s + 1))
                if cross is not None:
                    go(cross((sign * s) % NZ, c))

    for d in (1, 3, 2):
        go(ay(0, d))
    go(bz(0, 0, 1))
    go(bz(0, 1, 1))
    target(0, 5)
    ring(bz, 1)
    for d in (1, 2, 3):
        ay(-d, d).wait_recv()
    go(az(0, 0, 1))
    go(az(0, 1, 1))
    go(ac(0, c))
    target(5, 10)
    ring(bz, 2)
    target(10, 15)
    ring(bz, 3)
    ring(az, 1, ac)
    target(15, 20)
    ring(bz, 4)
    for d in (1, 3, 2):
        go(by(0, d))
    go(bc(0, c))
    target(20, 27)
    ring(az, 2, ac)
    target(27, 37)
    ring(az, 3, ac)
    target(37, 48)
    ring(az, 4, ac)
    for d in (1, 3, 2):
        by(-d, d).wait_recv()
        go(bc((-d) % NY, c))
    for k in range(NZ):
        ac(k, 1 - c).wait_recv()
    for k in range(NY):
        bc(k, 1 - c).wait_recv()

    kinds = [(per, first) for _, _, per, first in GROUPS]
    kinds += [(per, 12 + first % 4) for _, _, per, first in GROUPS]
    height = sum(16 * per for per, _ in kinds)
    row = lax.broadcasted_iota(jnp.int32, (height, 256), 0)
    col = lax.broadcasted_iota(jnp.int32, (height, 256), 1)
    pick = jnp.zeros((height, 256), jnp.int32)
    begins, start = [], 0
    for per, first in kinds:
        i = row - start
        here = (i >= 0) & (i < 16 * per)
        pick = jnp.where(here, (i // per) * 16 + first + lax.rem(i, per), pick)
        begins.append(start)
        start += 16 * per
    perm = jnp.where(col == pick, 1.0, 0.0).astype(BF16)

    def unpack(k, yy):
        q = px(k)
        parts = []
        for cc in range(NC):
            for zz in range(NZ):
                at = jnp.where(q < 2, place_a(cc, zz, yy), place_b(cc, yy, zz)) + lax.rem(q, 2)
                parts.append(hp[at])
        rows = dot(perm, jnp.concatenate(parts, axis=0)).astype(BF16)
        for g, (unit, _, per, first) in enumerate(GROUPS):
            n, h = 8 * per, 256 * (first // 4)
            for cc in range(NC):
                here = pl.ds(pl.multiple_of(unit * UT + cc * NY * n + yy * n, 16), n)
                a, b = begins[g] + cc * n, begins[NG + g] + cc * n
                hc[q, here, 0:PW] = rows[a:a + n]
                hc[q, here, PW:DW] = rows[b:b + n, h:h + 256]

    @pl.loop(0, 3 * NY)
    def _(i):
        unpack(i // NY - 1, lax.rem(i, NY))

    def two(quarter, part, slot, i):
        first, n = HALVES[part]
        toks = slice(256 * i, 256 * i + 256)
        rows = pl.ds(pl.multiple_of(px(quarter) * QR + BR + first, 16), n)
        other = hc[px(-1 if slot == 0 else 1), toks, :]
        return dot(wv[rows, :], hc[x, toks, :], NT) + dot(wq[slot, BR + first:BR + first + n, :], other, NT)

    def p_copy(part, i):
        first, n = HALVES[part]
        here = pl.ds(first, n)
        return remote(psend.at[i, here], precv.at[i, here], ps, (part, i), to(dx=(1, -1)[part]))

    def h_wait(j):
        remote(h_at(j), h_at(j), ws, (1, j), to(dx=ways[j][0])).wait_recv()

    for part_ in range(2):
        h_wait(part_)
        for i in range(TOK // 256):
            first, n = HALVES[part_]
            psend[i, first:first + n, :] = two((1, -1)[part_], part_, (0, 2)[part_], i)
            go(p_copy(part_, i))

    @pl.loop(0, NY)
    def _(i):
        unpack(2, i)

    def numerators(b, i, total):
        toks = pl.ds(pl.multiple_of(i * 256, 256), 256)
        real = lax.broadcasted_iota(jnp.int32, (BR, 256), 0) + (x * QR + b * BR) < VL
        total = jnp.where(real, total, -1e30)
        top = jnp.max(total, axis=0, keepdims=True)
        shifted = jnp.exp(total - top)
        sraw[pl.ds(b, 1), toks] = top
        sraw[pl.ds(2 + b, 1), toks] = jnp.sum(shifted, axis=0, keepdims=True)
        shifted = shifted.astype(BF16)
        ex[x, b, 2 * i] = shifted[:, 0:128]
        ex[x, b, 2 * i + 1] = shifted[:, 128:256]

    def e_at(q, b, g):
        return ex.at[q, b, pl.ds(GROUPS[g][0], GROUPS[g][1])]

    def e_copy(q, b, g, way):
        at = e_at(q, b, g)
        return remote(at, at, es, (way, b, g), to(dx=1 if way == 0 else -1))

    def f_copy(q, b, g):
        at = e_at(q, b, g)
        return remote(at, at, fs, (b, g), to(dx=1 if b == 0 else -1))

    def e_send(b, g):
        go(e_copy(x, b, g, 0))
        go(e_copy(x, b, g, 1))

    def e_wait(b, g, way):
        e_copy(px(-1 if way == 0 else 1), b, g, way).wait_recv()

    def e_forward(b, g):
        e_wait(b, g, b)
        go(f_copy(px(-1 if b == 0 else 1), b, g))

    for d in (1, 2, 3):
        at = wq.at[d - 1, pl.ds(0, BR)]
        remote(at, at, ws, (0, d - 1), to(dx=d)).wait_recv()

    @pl.loop(0, TOK // 256)
    def _(i):
        toks = pl.ds(pl.multiple_of(i * 256, 256), 256)
        total = dot(wv[pl.ds(pl.multiple_of(x * QR, 16), BR), :], hc[x, toks, :], NT)
        for d in (1, 2, 3):
            total += dot(wq[d - 1, 0:BR, :], hc[px(-d), toks, :], NT)
        numerators(0, i, total)

    h_wait(2)
    h_wait(3)
    for i in range(TOK // 256):
        for part_ in range(2):
            first, n = HALVES[part_]
            gw[i * BR + first:i * BR + first + n, 0:256] = two(0, part_, (2, 0)[part_], i)
    for i in range(0, 3 * QR, 128):
        pieces_, j = [], i
        while j < min(i + 128, 3 * QR):
            k = j // QR
            n = min(i + 128, 3 * QR, (k + 1) * QR) - j
            pieces_.append(wv[pl.ds(pl.multiple_of(px(slots[k]) * QR + j - k * QR, 16), n), :])
            j += n
        wta[:, i:j] = jnp.concatenate(pieces_, axis=0).T
    for i in range(0, QR, 128):
        n = min(128, QR - i)
        wtb[:, i:i + n] = wv[pl.ds(pl.multiple_of(px(2) * QR + i, 16), n), :].T

    for i in range(TOK // 256):
        for part_ in range(2):
            p_copy(part_, i).wait_recv()
    e_send(0, 0)

    @pl.loop(0, TOK // 256)
    def _(i):
        numerators(1, i, gw[pl.ds(pl.multiple_of(i * BR, 8), BR), 0:256] + precv[i])


    def sx_copy(q, d):
        return remote(sown, sx.at[q], sxs, (d - 1,), to(dx=d))

    for j in range(4):
        sown[j * NU:(j + 1) * NU, :] = fold(sraw[pl.ds(j, 1), :])
    for d in (1, 3, 2):
        go(sx_copy(x, d))
    e_send(1, 0)
    sx[x] = sown[...]
    for d in (1, 3, 2):
        sx_copy(px(-d), d).wait_recv()
    tops = [sx[q, b * NU:(b + 1) * NU, :] for q in range(NX) for b in range(2)]
    sums = [sx[q, (2 + b) * NU:(3 + b) * NU, :] for q in range(NX) for b in range(2)]

    def merge(tops, sums):
        top = functools.reduce(jnp.maximum, tops)
        return top, functools.reduce(jnp.add, [s * jnp.exp(t - top) for s, t in zip(sums, tops)])

    def spread(buf, sems, me, top, total, moves, slot, between):
        buf[me] = jnp.zeros((16, UT), F32)
        buf[me, 0:NU, :] = top
        buf[me, NU:2 * NU, :] = total
        for i, move in enumerate(moves):
            go(remote(buf.at[me], buf.at[me], sems, (i,), to(**move)))
        between()
        for i, move in enumerate(moves):
            at = buf.at[slot(move)]
            remote(at, at, sems, (i,), to(**move)).wait_recv()
        n = len(moves) + 1
        return merge([buf[k, 0:NU, :] for k in range(n)], [buf[k, NU:2 * NU, :] for k in range(n)])

    e_forward(0, 0)
    top, total = merge(tops, sums)
    top, total = spread(scr, scs, c, top, total, [dict(dc=1)], lambda m: 1 - c, lambda: None)

    def between_z():
        e_forward(1, 0)
        e_send(0, 1)

    def between_y():
        e_send(1, 1)

    moves = [dict(dz=d) for d in (4, 3, 5, 2, 6, 1, 7)]
    top, total = spread(sz, szs, z, top, total, moves, lambda m: pz(-m["dz"]), between_z)
    moves = [dict(dy=d) for d in (2, 1, 3)]
    top, total = spread(sy, sys_, y, top, total, moves, lambda m: py(-m["dy"]), between_y)
    scale = vec[0:NU, :] / total
    for i in range(2 * NX):
        fac[i, 0:NU, :] = scale * jnp.exp(tops[i] - top)

    def part(g, far):
        unit, units, _, _ = GROUPS[g]
        size, lane = units * UT, (256, 0, 256, 384)[g]
        for k in (3,) if far else (0, 1, 2):
            q = px(slots[k])
            if k == 3:
                f_copy(q, 0, g).wait_recv()
                f_copy(q, 1, g).wait_recv()
            elif k != 0:
                e_wait(2 - k, g, k - 1)
            for b in range(2):
                rows = pl.ds(pl.multiple_of(q * QR + b * BR, 16), BR)
                for u in range(units):
                    toks = pl.ds((unit + u) * UT, UT)
                    e = ex[q, b, unit + u].astype(F32)
                    score = fac[2 * q + b, pl.ds(unit + u, 1), :] * e - tgt[rows, toks].astype(F32)
                    here = k * QR + b * BR
                    st[here:here + BR, lane + u * UT:lane + (u + 1) * UT] = score.astype(BF16)

        @pl.loop(0, 2)
        def _(i):
            at = pl.ds(pl.multiple_of(i * HD, HD), HD)
            held = gp[(0, 0, 1, 0)[g]]
            if far:
                total = held[at, 0:size] + dot(wtb[at, :], st[3 * QR:VP, lane:lane + size])
                gt[g][:, at] = total.T
            else:
                held[at, 0:size] = dot(wta[at, :], st[0:3 * QR, lane:lane + size])

    def gw_part(g, k):
        rows = slice(k * QR, (k + 1) * QR)
        if g == 0:
            gw[rows, :] = dot(st[rows, 256:512], hc[x, 0:256, :])
        else:
            term = dot(st[rows, :], hc[x, 256:TOK, :])
            wv[rows, :] = (gw[rows, :] + term).astype(BF16)
            there = pl.ds(pl.multiple_of(px(slots[k]) * QR, 16), QR)
            copy = pltpu.make_async_copy(wv.at[pl.ds(k * QR, QR)], gw_ref.at[there], go_sem.at[k])
            copy.start()
            return copy

    def cores(g, cc):
        n = GROUPS[g][1] * UT // 2
        return pl.ds(pl.multiple_of(cc * n, 64), n)

    def tall(g):
        return GROUPS[g][2] * 8

    def deep(g, zz):
        return pl.ds(pl.multiple_of(zz * 8, 8), 8), pl.ds(0, DW * GROUPS[g][2] // 8)

    def r1(g):
        return remote(gt[g].at[cores(g, 1 - c)], cb[g], r1s, (g,), to(dc=1))

    def r2(g, d):
        n = tall(g)
        src = ysb[g].at[pl.ds(pl.multiple_of(py(d) * n, 16), n)]
        return remote(src, yb.at[g, d - 1, pl.ds(0, n)], r2s, (g, d - 1), to(dy=d))

    def r3(g, d):
        return remote(zsum.at[(g, *deep(g, pz(d)))], zb.at[(g, d - 1, *deep(g, 0))], r3s, (g, d - 1), to(dz=d))

    def start1(g):
        go(r1(g))

    def start2(g):
        r1(g).wait_recv()
        total = gt[g][cores(g, c), :] + cb[g][...]
        cb[g][...] = total
        ysb[g][...] = total.astype(BF16)
        for d in (1, 3, 2):
            go(r2(g, d))

    def start3(g):
        n, per = tall(g), GROUPS[g][2]
        for d in (1, 3, 2):
            r2(g, d).wait_recv()
        mine = cb[g][pl.ds(pl.multiple_of(y * n, 8), n), :]
        term = mine + functools.reduce(jnp.add, [yb[g, d, 0:n].astype(F32) for d in range(3)])
        w = DW * per // 8
        for zz in range(NZ):
            for k in range(8 // per):
                zsum[g, 8 * zz + per * k:8 * zz + per * (k + 1), 0:w] = term[per * zz:per * (zz + 1), w * k:w * (k + 1)]
        for d in (4, 3, 5, 2, 6, 1, 7):
            go(r3(g, d))

    def finish(g):
        _, _, per, first = GROUPS[g]
        for d in range(1, NZ):
            r3(g, d).wait_recv()
        term = zsum[(g, *deep(g, z))]
        for d in range(1, NZ):
            term += zb[(g, d - 1, *deep(g, 0))]
        w = DW * per // 8
        for k in range(8 // per):
            outf[first:first + per, w * k:w * (k + 1)] = term[per * k:per * (k + 1)]

    e_forward(0, 1)
    part(0, False)
    e_send(0, 2)
    part(0, True)
    start1(0)
    e_send(1, 2)
    gw_part(0, 0)
    gw_part(0, 1)
    e_forward(1, 1)
    e_send(0, 3)
    gw_part(0, 2)
    gw_part(0, 3)
    start2(0)
    e_send(1, 3)
    part(1, False)
    e_forward(0, 2)
    e_forward(1, 2)
    part(2, False)
    part(1, True)
    start1(1)
    e_forward(0, 3)
    e_forward(1, 3)
    start2(1)
    part(3, False)
    part(2, True)
    start1(2)
    start3(0)
    for copy in loaded:
        copy.wait_send()
    part(3, True)
    start1(3)
    start2(2)
    start3(1)
    outs = [gw_part(2, 0)]
    start2(3)
    outs.append(gw_part(2, 1))
    start3(2)
    outs.append(gw_part(2, 2))
    start3(3)
    outs.append(gw_part(2, 3))
    finish(0)
    finish(1)
    finish(2)
    finish(3)
    ghs[...] = outf[0:12, :].astype(BF16)
    outs.append(pltpu.make_async_copy(ghs, gh_ref, go_sem.at[NX]))
    outs[-1].start()
    for copy in outs:
        copy.wait()
    for copy in pending:
        copy.wait_send()


def results(gw_ref, gh_ref, gw_out, gh_out, sems):
    copies = [pltpu.make_async_copy(gh_ref, gh_out, sems.at[5])]
    for i, (start, rows) in enumerate(((0, QR), (QR, QR), (2 * QR, QR), (3 * QR, 2368 - 3 * QR), (2368, VL - 2368))):
        here = pl.ds(start, rows)
        copies.append(pltpu.make_async_copy(gw_ref.at[here], gw_out.at[here], sems.at[i]))
    for copy in copies:
        copy.start()
    for copy in copies:
        copy.wait()


def local(hidden, head_weight, teacher_ids, teacher_probs, token_weight):
    hbm = pl.BlockSpec(memory_space=pl.ANY)
    dma = pltpu.SemaphoreType.DMA
    gw, gh = pl.pallas_call(
        kernel,
        grid=(1,),
        out_shape=(pltpu.VMEM((VP, DW), BF16), pltpu.VMEM((12, DW), BF16)),
        in_specs=[
            pl.BlockSpec((12, DW), lambda i: (0, 0)),
            pl.BlockSpec((16, DW), lambda i: (2368 // 16, 0)),
            hbm, hbm, hbm, hbm,
        ],
        out_specs=(hbm, hbm),
        scratch_shapes=[
            pltpu.VMEM((VP, DW), BF16),
            pltpu.VMEM((3, QR, DW), BF16),
            pltpu.VMEM((DW, 3 * QR), BF16),
            pltpu.VMEM((DW, QR), BF16),
            pltpu.VMEM((16, PW), BF16),
            pltpu.VMEM((256, 16, PW), BF16),
            pltpu.VMEM((NX, TOK, DW), BF16),
            pltpu.VMEM((NX, 2, TOK // UT, BR, UT), BF16),
            pltpu.VMEM((VP, TOK), BF16),
            pltpu.VMEM((VP, 512), BF16),
            pltpu.VMEM((VP, DW), F32),
            [pltpu.VMEM((DW, n), F32) for n in (256, 128)],
            [pltpu.VMEM((n * UT, DW), F32) for _, n, _, _ in GROUPS],
            [pltpu.VMEM((n * UT // 2, DW), F32) for _, n, _, _ in GROUPS],
            [pltpu.VMEM((n * UT // 2, DW), BF16) for _, n, _, _ in GROUPS],
            pltpu.VMEM((NG, 3, 32, DW), BF16),
            pltpu.VMEM((NG, 64, HD), F32),
            pltpu.VMEM((NG, 7, 8, HD), F32),
            pltpu.VMEM((16, DW), F32),
            pltpu.VMEM((12, DW), BF16),
            pltpu.VMEM((TOK // 256, BR, 256), F32),
            pltpu.VMEM((TOK // 256, BR, 256), F32),
            pltpu.VMEM((8, TOK), F32),
            pltpu.VMEM((4 * NU, UT), F32),
            pltpu.VMEM((NX, 4 * NU, UT), F32),
            pltpu.VMEM((NC, 16, UT), F32),
            pltpu.VMEM((NZ, 16, UT), F32),
            pltpu.VMEM((NY, 16, UT), F32),
            pltpu.VMEM((2 * NX, 8, UT), F32),
            pltpu.VMEM((TOPK, TOK), jnp.int32),
            pltpu.VMEM((TOPK, TOK), F32),
            pltpu.VMEM((TOK,), F32),
            pltpu.VMEM((TOPK, TOK), jnp.int32),
            pltpu.VMEM((TOPK, TOK), F32),
            pltpu.VMEM((8, UT), F32),
            dma((4,)), dma((3,)), dma((5,)),
            dma((2, 3)), dma((2, 2, 4)), dma((2, 2, 3)), dma((2, 3)), dma((2, 2, 4)), dma((2, 2, 4)), dma((2, 3)), dma((2, 8)),
            dma((2, 4)), dma((2, 2, 2, NG)), dma((2, 2, NG)), dma((2, 3)), dma((2, 1)), dma((2, 7)), dma((2, 3)),
            dma((2, NG)), dma((2, NG, 3)), dma((2, NG, 7)),
        ],
        compiler_params=pltpu.CompilerParams(
            collective_id=0, has_side_effects=True, vmem_limit_bytes=117 * 2**19
        ),
        name="head_backward",
    )(hidden, head_weight, head_weight, teacher_ids.T, teacher_probs.T, token_weight)
    gw, gh = pl.pallas_call(
        results,
        out_shape=(jax.ShapeDtypeStruct((VL, DW), BF16), jax.ShapeDtypeStruct((12, DW), BF16)),
        in_specs=[hbm, hbm],
        out_specs=(hbm, hbm),
        scratch_shapes=[dma((6,))],
        compiler_params=pltpu.CompilerParams(vmem_limit_bytes=2**20),
        name="results",
    )(gw, gh)
    return gh, gw


def solution(mesh):
    return jax.shard_map(
        local,
        mesh=mesh,
        in_specs=(P("vocab", "hid"), P("vocab", "hid"), P(), P(), P()),
        out_specs=(P("vocab", "hid"), P("vocab", "hid")),
        check_vma=False,
    )
```
